32 devices in a mesh: rep: 8 (over z, x), layer: 4 (over y, core).
Axes of the slice: x: 2, y: 2, z: 4, core: 2. Of those that a mesh axis runs over, the one named last changes fastest.
Arguments:
- activations: bfloat16 [4, 4096, 8192], P('layer', 'rep'), may hold values from -6 to 6
- output_grads: bfloat16 [4, 4096, 8192], P('layer', 'rep'), may hold values from -6 to 6
- in_projection: bfloat16 [4, 32, 8192], P('layer'), may hold values from -0.0625 to 0.0625
- out_projection: bfloat16 [4, 32, 8192], P('layer'), may hold values from -0.0625 to 0.0625
- segment_ids: int32 [4096], P('rep'), may hold values from -1 to 61, as said below
- move_list: int32 [496], P('rep'), may hold values from -1 to 255, as said below
Outputs:
- factor: float32 [4, 1024, 1024], P('layer')
- features: bfloat16 [4, 256, 1024], P('layer', 'rep')
- self_influence: float32 [256], P('rep')
The draws below stay inside these ranges and needn't reach their ends.
Inputs may be any that keep to these rules, and one draw needn't show every extreme that they name: `segment_ids`: within each replica's 512 tokens the values never fall; a run of equal values is one document; -1 marks tokens continuing the previous replica's last document and never occurs on replica 0; n documents start on a replica with values 0 to n - 1, n from 2 to 62, and some replica has exactly 62; all documents together are 256; the last document ends at the end of the last replica. `move_list`: replica r's block of 62 entries gives for its documents in order of their first token (the one continuing onto replica r + 1 included) the destination row in 0 to 255, and -1 past its last document; every row is named exactly once; the documents of replica r go to rows of replica r - 1, r or r + 1 (rows m * 32 to m * 32 + 31 belong to replica m).
All inputs are finite; a program needn't handle non-finite values.
Results may differ from the reference program's by a relative error of at most 0.0064.
Values may be sent and summed in bfloat16 or wider, within the bound.
No kernel may reach another device: no remote copies, remote signals or barrier semaphores. Data moves between devices by JAX's collectives and lax.ppermute only.
A program may use at most 128 MiB of HBM per device.

```python
import jax
import jax.numpy as jnp
from jax import lax

D = 8192
KIN = 32
KOUT = 32
TOK_DEV = 512
BAL = 32
DSLOT = 62
LAYERS = 4
TOKENS = 4096
DOCS = 256
N_REP = 8


def make_plan(key):
    base = jax.random.fold_in(key, 11)
    key_drift, key_peak, key_place, key_rows = jax.random.split(base, 4)
    spread = BAL // 2 - 1
    drifts = jax.random.randint(key_drift, (N_REP + 1,), -spread, spread + 1)
    peak_rep = jax.random.randint(key_peak, (), 1, N_REP - 1)
    edge_idx = jnp.arange(N_REP + 1, dtype=jnp.int32)
    drifts = jnp.where(edge_idx == peak_rep, -spread, drifts)
    drifts = jnp.where(edge_idx == peak_rep + 1, spread, drifts)
    drifts = jnp.where((edge_idx == 0) | (edge_idx == N_REP), 0, drifts)
    doc_counts = BAL + drifts[1:] - drifts[:-1]
    place_keys = jax.random.split(key_place, N_REP)
    shuffled = jax.vmap(lambda subkey: jax.random.permutation(subkey, TOK_DEV))(place_keys)
    ranking = jnp.argsort(shuffled, axis=1).astype(jnp.int32)
    rank_zero = ranking[:, :1]
    token_pos = jnp.arange(TOK_DEV, dtype=jnp.int32)[None, :]
    moved_rank = jnp.where(token_pos == 0, 0, ranking + (ranking < rank_zero).astype(jnp.int32))
    rep_index = jnp.arange(N_REP, dtype=jnp.int32)[:, None]
    ranking = jnp.where(rep_index == 0, moved_rank, ranking)
    starts = ranking < doc_counts[:, None]
    segment = jnp.cumsum(starts.astype(jnp.int32), axis=1) - 1
    first_doc = jnp.arange(N_REP, dtype=jnp.int32) * BAL + drifts[:-1]
    doc_slot = jnp.arange(DSLOT, dtype=jnp.int32)[None, :]
    global_id = first_doc[:, None] + doc_slot
    row_keys = jax.random.split(key_rows, N_REP)
    inner_rows = jax.vmap(lambda subkey: jax.random.permutation(subkey, BAL))(row_keys).astype(jnp.int32)

    def natural_target(doc_ids):
        dest_rep = jnp.clip(doc_ids // BAL, 0, N_REP - 1)
        inside = jnp.clip(doc_ids - dest_rep * BAL, 0, BAL - 1)
        return dest_rep * BAL + inner_rows[dest_rep, inside]
    reps = jnp.arange(N_REP, dtype=jnp.int32)
    low_own = reps * BAL + jnp.maximum(drifts[:-1], 0)
    high_own = (reps + 1) * BAL - 1 + jnp.minimum(drifts[1:], 0)
    next_low = jnp.concatenate([low_own[1:], low_own[:1]])
    prev_high = jnp.concatenate([high_own[-1:], high_own[:-1]])
    rep_col = reps[:, None]
    target = natural_target(global_id)
    to_right = (global_id == high_own[:, None]) & (rep_col < N_REP - 1)
    to_left = (global_id == low_own[:, None]) & (rep_col > 0)
    target = jnp.where(to_right, natural_target(next_low)[:, None], target)
    target = jnp.where(to_left, natural_target(prev_high)[:, None], target)
    moves = jnp.where(doc_slot < doc_counts[:, None], target, -1)
    return (segment.reshape(-1).astype(jnp.int32), moves.reshape(-1).astype(jnp.int32))


def draw_segment_ids(key, part):
    segment, moves = make_plan(key)
    return segment


def draw_move_list(key, part):
    segment, moves = make_plan(key)
    return moves


def levels(key, dims, cuts, low, top_value):
    gain = 1.0
    for dim, blocks in cuts:
        steps = jax.random.uniform(jax.random.fold_in(jax.random.fold_in(key, 6), dim), (blocks,), jnp.float32, low / len(cuts), top_value / len(cuts))
        gain = gain * jnp.repeat(jnp.exp(steps), dims[dim] // blocks).reshape((-1,) + (1,) * (len(dims) - 1 - dim))
    return gain


def normal_values(stream_key, dims, scale, bound, cuts=(), held_as=jnp.bfloat16):
    drawn = scale * jax.random.normal(stream_key, dims, jnp.float32)
    if cuts:
        drawn = drawn * levels(stream_key, dims, cuts, -0.22, 0.18)
    return jnp.clip(drawn, -bound, bound).astype(held_as)


def setup_inputs(seed: int = 0) -> dict:
    streams_of = jax.random.split(jax.random.key(seed), 7)
    return {
        "activations": normal_values(streams_of[0], (LAYERS, TOKENS, D), 1.0, 6.0, ((0, 4), (1, 8))),
        "output_grads": normal_values(streams_of[1], (LAYERS, TOKENS, D), 1.0, 6.0, ((0, 4), (1, 8))),
        "in_projection": normal_values(streams_of[2], (LAYERS, KIN, D), D ** -0.5, 0.0625, ((0, 4),)),
        "out_projection": normal_values(streams_of[3], (LAYERS, KOUT, D), D ** -0.5, 0.0625, ((0, 4),)),
        "segment_ids": draw_segment_ids(jax.random.fold_in(streams_of[6], 71), 0),
        "move_list": draw_move_list(jax.random.fold_in(streams_of[6], 71), 0),
    }


DAMPING = 0.05

def layer_terms(acts_layer, grads_layer, proj_in, proj_out, segment_ids, move_list):
    width = KIN * KOUT
    left = jnp.dot(acts_layer.astype(jnp.float32), proj_in.T.astype(jnp.float32), preferred_element_type=jnp.float32).astype(jnp.bfloat16)
    right = jnp.dot(grads_layer.astype(jnp.float32), proj_out.T.astype(jnp.float32), preferred_element_type=jnp.float32).astype(jnp.bfloat16)
    outer = (left.astype(jnp.float32)[:, :, None] * right.astype(jnp.float32)[:, None, :]).reshape(TOKENS, width)
    positions = jnp.arange(TOKENS, dtype=jnp.int32) % TOK_DEV
    previous = jnp.concatenate([segment_ids[:1], segment_ids[:-1]])
    starts = (segment_ids >= 0) & ((positions == 0) | (segment_ids != previous))
    doc_index = jnp.cumsum(starts.astype(jnp.int32)) - 1
    sums = jax.ops.segment_sum(outer, doc_index, num_segments=DOCS)
    lengths = jax.ops.segment_sum(jnp.ones((TOKENS,), jnp.float32), doc_index, num_segments=DOCS)
    doc_features = (sums / jnp.sqrt(lengths)[:, None]).astype(jnp.bfloat16)
    valid = move_list >= 0
    entry_doc = jnp.cumsum(valid.astype(jnp.int32)) - 1
    target = jnp.where(valid, move_list, DOCS).astype(jnp.int32)
    source = jnp.clip(entry_doc, 0, DOCS - 1).astype(jnp.int32)
    placed = jnp.zeros((DOCS, width), jnp.bfloat16).at[target].set(doc_features[source], mode='drop')
    gram = lax.dot_general(placed.astype(jnp.float32), placed.astype(jnp.float32), (((0,), (0,)), ((), ())), preferred_element_type=jnp.float32)
    hessian = gram / DOCS + DAMPING * jnp.eye(width, dtype=jnp.float32)
    lower = jnp.linalg.cholesky(hessian)
    solved = lax.linalg.triangular_solve(lower, placed.T.astype(jnp.float32), left_side=True, lower=True)
    quad = lax.optimization_barrier(jnp.sum(solved * solved, axis=0)) / width
    return (lower.T, placed, quad)

def reference(activations, output_grads, in_projection, out_projection, segment_ids, move_list):
    factors = []
    placed_all = []
    influence = jnp.zeros((DOCS,), jnp.float32)
    for layer_id in range(LAYERS):
        upper, placed, quad = layer_terms(activations[layer_id], output_grads[layer_id], in_projection[layer_id], out_projection[layer_id], segment_ids, move_list)
        factors.append(upper)
        placed_all.append(placed)
        influence = influence + quad
    return (jnp.stack(factors), jnp.stack(placed_all), influence)
```

```python
import functools

import jax
import jax.numpy as jnp
from jax import lax
from jax.experimental import pallas as pl
from jax.experimental.pallas import tpu as pltpu
from jax.sharding import PartitionSpec as P

BAL = 32
DAMPING = 0.05
BLK = 128
PAN = 256
EXACT = lax.Precision.HIGHEST


def shifted(block, axis, distance):
    devices = range(lax.axis_size(axis))
    route = [(i - distance, i) for i in devices if i - distance in devices]
    return lax.ppermute(block, axis, route)


def swapped(block, axis, distance):
    devices = range(lax.axis_size(axis))
    return lax.ppermute(block, axis, [(i, i ^ distance) for i in devices])


def gathered(block, axis):
    pair = jnp.stack([block, swapped(block, axis, 1)])
    rest = [swapped(pair, axis, d) for d in range(2, lax.axis_size(axis), 2)]
    return jnp.concatenate([pair, *rest])


def lane_of(v, j):
    return jnp.broadcast_to(v[:, j : j + 1], v.shape)


def row_of(v, s):
    return jnp.broadcast_to(v[s : s + 1, :], v.shape)


def factor_block(x, u_ref, m_ref):
    x = list(x)
    lane = lax.broadcasted_iota(jnp.int32, (8, BLK), 1)
    sub = lax.broadcasted_iota(jnp.int32, (8, BLK), 0)
    groups = BLK // 8
    for t in range(groups):
        cols = [[lane_of(x[i], 8 * t + c) for c in range(8)] for i in range(t, groups)]
        inside = (lane >= 8 * t) & (lane < 8 * t + 8)
        own, here, rows = cols[0], x[t], []
        for c in range(8):
            j = 8 * t + c
            inv = 1.0 / row_of(own[c], c)
            row = jnp.where(lane == j, 1.0, row_of(here, c)) * inv
            rows.append(jnp.where(inside & (lane > j), 0.0, row))
            mult = jnp.where(sub > c, own[c], 0.0)
            here = jnp.where((lane == j) & (sub > c), 0.0, here) - mult * row
            weights = {k: row_of(own[k], c) * inv for k in range(c + 1, 8)}
            for i in range(1, len(cols)):
                for k in range(c + 1, 8):
                    cols[i][k] = cols[i][k] - cols[i][c] * weights[k]
            own = [own[k] - mult * weights[k] if k > c else own[k] for k in range(8)]
        x[t] = here
        for i in range(t + 1, groups):
            total = jnp.where(inside, 0.0, x[i])
            for c in range(8):
                total = total - cols[i - t][c] * rows[c]
            x[i] = total
    for i in range(groups):
        row = 8 * i + sub
        pivot = jnp.sum(jnp.where(lane == row, x[i], 0.0), axis=1, keepdims=True)
        scale = lax.rsqrt(jnp.broadcast_to(pivot, (8, BLK)))
        scaled = x[i] * scale
        u_ref[8 * i : 8 * i + 8, :] = jnp.where(lane >= row, scaled, 0.0)
        m_ref[8 * i : 8 * i + 8, :] = jnp.where(
            lane < row, scaled, jnp.where(lane == row, scale, 0.0)
        )


def dot(a, b):
    return jnp.dot(a, b, precision=EXACT, preferred_element_type=jnp.float32)


def dot_t(a, b, precision=EXACT):
    return lax.dot_general(
        a, b, (((0,), (0,)), ((), ())), precision=precision, preferred_element_type=jnp.float32
    )


def groups_of(block):
    return [block[8 * i : 8 * i + 8, :] for i in range(BLK // 8)]


def cholesky_kernel(width, place_ref, blocks_ref, u_out, quad_ref, f_ref, u_ref, s_ref, m_ref, sems):
    n_rep, rows, _ = blocks_ref.shape
    docs = n_rep * rows
    wide = width + BLK
    me = place_ref[0]
    for d in range(n_rep):
        at = pl.multiple_of((me ^ d) * rows, rows)
        f_ref[pl.ds(at, rows), 0:width] = blocks_ref[d]
    doc = lax.broadcasted_iota(jnp.int32, (docs, BLK), 0)
    slot = lax.broadcasted_iota(jnp.int32, (docs, BLK), 1)
    f_ref[:, width:] = jnp.where((doc == me * rows + slot) & (slot < rows), 1.0, 0.0).astype(
        jnp.bfloat16
    )
    eye = jnp.where(
        lax.broadcasted_iota(jnp.int32, (PAN, PAN), 0) == lax.broadcasted_iota(jnp.int32, (PAN, PAN), 1),
        DAMPING,
        0.0,
    )
    copies = []
    for k in range(width // PAN):
        a, b, c = PAN * k, PAN * k + BLK, PAN * k + PAN
        left = f_ref[:, a:c]
        gram = dot_t(left, f_ref[:, a:width], None) * (1.0 / docs)
        own = dot_t(left, f_ref[:, width:], None)
        if k:
            done = u_ref[0:a, a:c]
            gram = gram - dot_t(done, u_ref[0:a, a:width])
            own = own - dot_t(done, u_ref[0:a, width:])
            u_ref[a:c, 0:a] = jnp.zeros((PAN, a), jnp.float32)
        s_ref[:, a:c] = gram[:, 0:PAN] + eye
        if c < width:
            s_ref[:, c:width] = gram[:, PAN:]
        s_ref[:, width:] = own
        factor_block(groups_of(s_ref[0:BLK, a:b]), u_ref.at[a:b, a:b], m_ref.at[0])
        upper = dot(m_ref[0], s_ref[0:BLK, b:])
        u_ref[a:b, b:] = upper
        u_ref[b:c, a:b] = jnp.zeros((BLK, BLK), jnp.float32)
        corner = s_ref[BLK:, b:c] - dot_t(upper[:, 0:BLK], upper[:, 0:BLK])
        factor_block(groups_of(corner), u_ref.at[b:c, b:c], m_ref.at[1])
        rest = s_ref[BLK:, c:] - dot_t(upper[:, 0:BLK], upper[:, BLK:])
        u_ref[b:c, c:] = dot(m_ref[1], rest)
        copy = pltpu.make_async_copy(u_ref.at[a:c, 0:width], u_out.at[a:c, :], sems.at[k])
        copy.start()
        copies.append(copy)
    solved = u_ref[:, width:]
    quad = jnp.sum(solved * solved, axis=0, keepdims=True) * (1.0 / width)
    quad_ref[...] = jnp.broadcast_to(quad, quad_ref.shape)
    for copy in copies:
        copy.wait()


def factor_and_solve(blocks, replica):
    n_rep, rows, width = blocks.shape
    vmem = pl.BlockSpec(memory_space=pltpu.VMEM)
    upper, quad = pl.pallas_call(
        functools.partial(cholesky_kernel, width),
        out_shape=[
            jax.ShapeDtypeStruct((width, width), jnp.float32),
            jax.ShapeDtypeStruct((8, BLK), jnp.float32),
        ],
        in_specs=[pl.BlockSpec(memory_space=pltpu.SMEM), vmem],
        out_specs=[pl.BlockSpec(memory_space=pl.ANY), vmem],
        scratch_shapes=[
            pltpu.VMEM((n_rep * rows, width + BLK), jnp.bfloat16),
            pltpu.VMEM((width, width + BLK), jnp.float32),
            pltpu.VMEM((PAN, width + BLK), jnp.float32),
            pltpu.VMEM((2, BLK, BLK), jnp.float32),
            pltpu.SemaphoreType.DMA((width // PAN,)),
        ],
        compiler_params=pltpu.CompilerParams(vmem_limit_bytes=40 * 1024 * 1024),
        name="cholesky",
    )(jnp.reshape(replica, (1,)).astype(jnp.int32), blocks)
    return upper, quad[0, :rows]


def on_device(activations, output_grads, in_projection, out_projection, segment_ids, move_list):
    contract = (((1,), (1,)), ((), ()))
    left = lax.dot_general(
        in_projection[0], activations[0], contract, preferred_element_type=jnp.float32
    ).astype(jnp.bfloat16)
    right = lax.dot_general(
        out_projection[0], output_grads[0], contract, preferred_element_type=jnp.float32
    ).astype(jnp.bfloat16)
    doc_slots = move_list.shape[0]
    width = left.shape[0] * right.shape[0]
    slot_ids = jnp.arange(doc_slots + 1, dtype=jnp.int32) - 1
    member = (segment_ids[None, :] == slot_ids[:, None]).astype(jnp.bfloat16)
    masked = member[:, None, :] * left[None, :, :]
    blocks = lax.dot_general(
        masked, right, (((2,), (1,)), ((), ())), preferred_element_type=jnp.float32
    )
    sums = blocks.reshape(doc_slots + 1, width)
    counts = jnp.sum(member.astype(jnp.float32), axis=1)
    carried_sum, carried_count = shifted((sums[:1], counts[:1]), "rep", -1)
    last_slot = jnp.max(segment_ids)
    takes = (slot_ids[1:] == last_slot).astype(jnp.float32)
    totals = sums[1:] + takes[:, None] * carried_sum
    lengths = counts[1:] + takes * carried_count[0]
    safe_len = jnp.maximum(lengths, 1.0)
    local_features = (totals / jnp.sqrt(safe_len)[:, None]).astype(jnp.bfloat16)
    replica = lax.axis_index("rep")
    offsets = jnp.where(move_list >= 0, move_list // BAL - replica, 5)
    within = move_list % BAL
    row_ids = jnp.arange(BAL, dtype=jnp.int32)

    def arrange(step_offset):
        select = ((offsets[None, :] == step_offset) & (within[None, :] == row_ids[:, None])).astype(
            jnp.bfloat16
        )
        return jnp.dot(select, local_features, preferred_element_type=jnp.float32).astype(
            jnp.bfloat16
        )

    staying = arrange(0)
    from_right = shifted(arrange(-1), "rep", -1)
    from_left = shifted(arrange(1), "rep", 1)
    mine = (
        staying.astype(jnp.float32) + from_right.astype(jnp.float32) + from_left.astype(jnp.float32)
    ).astype(jnp.bfloat16)
    upper, quad = factor_and_solve(gathered(mine, "rep"), replica)
    influence = lax.psum(quad, "layer")
    return (upper[None], mine[None], influence)


def solution(mesh):
    placed = (
        P("layer", "rep", None),
        P("layer", "rep", None),
        P("layer", None, None),
        P("layer", None, None),
        P("rep"),
        P("rep"),
    )
    return jax.shard_map(
        on_device,
        mesh=mesh,
        in_specs=placed,
        out_specs=(P("layer", None, None), P("layer", "rep", None), P("rep")),
        check_vma=False,
    )
```

```python
import functools

import jax
import jax.numpy as jnp
from jax import lax
from jax.experimental import pallas as pl
from jax.experimental.pallas import tpu as pltpu
from jax.sharding import PartitionSpec as P

BAL = 32
DAMPING = 0.05
BLK = 128
PAN = 256
SUP = 32
STEP = 16
EXACT = lax.Precision.HIGHEST
VMEM = pl.BlockSpec(memory_space=pltpu.VMEM)
FAR = pl.BlockSpec(memory_space=pltpu.HBM)


def swapped(block, axis, distance):
    devices = range(lax.axis_size(axis))
    return lax.ppermute(block, axis, [(i, i ^ distance) for i in devices])


def gathered(block, axis):
    even = [swapped(block, axis, d) for d in range(2, lax.axis_size(axis), 2)]
    pieces = [block, swapped(block, axis, 1)]
    for piece in even:
        pieces += [piece, swapped(piece, axis, 1)]
    return pieces


def lane_of(v, j):
    return jnp.broadcast_to(v[:, j : j + 1], v.shape)


def row_of(v, s):
    return jnp.broadcast_to(v[s : s + 1, :], v.shape)


def dot(a, b, precision=EXACT):
    return jnp.dot(a, b, precision=precision, preferred_element_type=jnp.float32)


def dot_t(a, b, precision=EXACT):
    return lax.dot_general(
        a, b, (((0,), (0,)), ((), ())), precision=precision, preferred_element_type=jnp.float32
    )


def dot_n(a, b):
    return lax.dot_general(a, b, (((1,), (1,)), ((), ())), preferred_element_type=jnp.float32)


def project_kernel(acts, grads, w_in, w_out, segments, moves, out, a_ref, g_ref, wi_ref, wo_ref, seg_ref, move_ref, sems):
    tokens, depth = a_ref.shape
    parts = sems.shape[0] // 2 - 2
    deep = depth // parts
    width = w_in.shape[0]
    small = [
        pltpu.make_async_copy(segments, seg_ref, sems.at[2 * parts]),
        pltpu.make_async_copy(moves, move_ref, sems.at[2 * parts + 1]),
    ]
    weights = [
        pltpu.make_async_copy(w_in, wi_ref, sems.at[2 * parts + 2]),
        pltpu.make_async_copy(w_out, wo_ref, sems.at[2 * parts + 3]),
    ]
    copies = []
    for c in range(parts):
        at = pl.ds(c * deep, deep)
        copies += [
            pltpu.make_async_copy(acts.at[:, at], a_ref.at[:, at], sems.at[2 * c]),
            pltpu.make_async_copy(grads.at[:, at], g_ref.at[:, at], sems.at[2 * c + 1]),
        ]
    for copy in [*small, *weights, *copies]:
        copy.start()
    for copy in small:
        copy.wait()
    slots = moves.shape[1]
    slot = lax.broadcasted_iota(jnp.int32, (slots, slots), 0)
    other = lax.broadcasted_iota(jnp.int32, (slots, slots), 1)
    column = jnp.sum(jnp.where(slot == other, move_ref[...], 0), axis=1, keepdims=True)
    segment = seg_ref[...]
    slot = lax.broadcasted_iota(jnp.int32, (slots, tokens), 0)
    target = jnp.sum(jnp.where(slot == segment, column, 0), axis=0, keepdims=True)
    target = jnp.where(segment < 0, -1, target)
    line = lax.broadcasted_iota(jnp.int32, (16, tokens), 0)
    coded = jnp.where(line == 0, target >> 5, jnp.where(line == 1, target & 31, 0))
    out[2 * width :, :] = coded.astype(jnp.float32).astype(jnp.bfloat16)
    for copy in weights:
        copy.wait()
    left = right = jnp.zeros((tokens, width), jnp.float32)
    for c in range(parts):
        at = slice(c * deep, c * deep + deep)
        copies[2 * c].wait()
        copies[2 * c + 1].wait()
        left = left + dot_n(a_ref[:, at], wi_ref[:, at])
        right = right + dot_n(g_ref[:, at], wo_ref[:, at])
    out[0:width, :] = left.T.astype(jnp.bfloat16)
    out[width : 2 * width, :] = right.T.astype(jnp.bfloat16)


def project(activations, output_grads, in_projection, out_projection, segment_ids, move_list):
    tokens, depth = activations.shape
    width = in_projection.shape[0]
    slots = move_list.shape[0]
    parts = depth // 512
    return pl.pallas_call(
        project_kernel,
        out_shape=jax.ShapeDtypeStruct((2 * width + 16, tokens), jnp.bfloat16),
        in_specs=[FAR] * 6,
        out_specs=VMEM,
        scratch_shapes=[
            pltpu.VMEM((tokens, depth), jnp.bfloat16),
            pltpu.VMEM((tokens, depth), jnp.bfloat16),
            pltpu.VMEM((width, depth), jnp.bfloat16),
            pltpu.VMEM((width, depth), jnp.bfloat16),
            pltpu.VMEM((1, tokens), jnp.int32),
            pltpu.VMEM((1, slots), jnp.int32),
            pltpu.SemaphoreType.DMA((2 * parts + 4,)),
        ],
        compiler_params=pltpu.CompilerParams(vmem_limit_bytes=58 * 1024 * 1024),
        name="project",
    )(
        activations,
        output_grads,
        in_projection,
        out_projection,
        segment_ids.reshape(1, tokens),
        move_list.reshape(1, slots),
    )


def eliminate(x, first):
    lane = lax.broadcasted_iota(jnp.int32, (8, BLK), 1)
    sub = lax.broadcasted_iota(jnp.int32, (8, BLK), 0)
    x, count, deep = list(x), len(x), STEP // 8
    scales = [None] * count
    for t in range(0, count, deep):
        lo = first + 8 * t
        cols = [[lane_of(x[t + q], lo + c) for q in range(deep)] for c in range(STEP)]
        below = {i: [lane_of(x[i], lo + c) for c in range(STEP)] for i in range(t + deep, count)}
        work = [x[t + q] for q in range(deep)]
        kept, pivots = list(work), [jnp.ones((8, BLK), jnp.float32)] * deep
        for c in range(STEP):
            own, s = divmod(c, 8)
            hit, at = sub == s, lane == lo + c
            pivot = row_of(cols[c][own], s)
            inv = 1.0 / pivot
            kept[own] = jnp.where(hit, work[own], kept[own])
            pivots[own] = jnp.where(hit, pivot, pivots[own])
            row = jnp.where(at, 1.0, row_of(work[own], s)) * inv
            for q in range(deep):
                new = jnp.where(at, 0.0, work[q]) - cols[c][q] * row
                work[q] = jnp.where(hit, row, new) if q == own else new
            for k in range(c + 1, STEP):
                raw = row_of(cols[k][own], s)
                weight = raw * inv
                for q in range(deep):
                    if k == c + 1:
                        new = cols[k][q] - (cols[c][q] * raw) * inv
                    else:
                        new = cols[k][q] - cols[c][q] * weight
                    cols[k][q] = jnp.where(hit, weight, new) if q == own else new
        inside = (lane >= lo) & (lane < lo + STEP)
        for i in range(t + deep, count):
            terms = [below[i][c] * row_of(work[c // 8], c % 8) for c in range(STEP)]
            while len(terms) > 1:
                terms = [terms[m] + terms[m + 1] for m in range(0, len(terms), 2)]
            x[i] = jnp.where(inside, 0.0, x[i]) - terms[0]
        for q in range(deep):
            scales[t + q] = lax.rsqrt(pivots[q])
            x[t + q] = kept[q] * scales[t + q]
    return x, scales


def factor_block(d_ref, u_ref, m_ref):
    lane = lax.broadcasted_iota(jnp.int32, (8, BLK), 1)
    sub = lax.broadcasted_iota(jnp.int32, (8, BLK), 0)
    tall_row = lax.broadcasted_iota(jnp.int32, (SUP, BLK), 0)
    tall_lane = lax.broadcasted_iota(jnp.int32, (SUP, BLK), 1)
    groups, n = BLK // 8, SUP // 8
    x = [d_ref[8 * i : 8 * i + 8, :] for i in range(groups)]
    for h in range(0, groups, n):
        a, b = 8 * h, 8 * (h + n)
        rows, scales = eliminate(x[h : h + n], a)
        if b < BLK:
            block, scale = jnp.concatenate(rows, 0), jnp.concatenate(scales, 0)
            row = tall_row + a
            right = jnp.where(
                (tall_lane > row) & (tall_lane < b), 0.0, jnp.where(tall_lane == row, scale, block)
            )
            update = dot_t(block, right)
            for i in range(h + n, groups):
                x[i] = jnp.where((lane >= a) & (lane < b), 0.0, x[i]) - update[8 * i : 8 * i + 8, :]
        for q in range(n):
            row = a + 8 * q + sub
            at = slice(a + 8 * q, a + 8 * q + 8)
            u_ref[at, :] = jnp.where(lane >= row, rows[q], 0.0)
            m_ref[at, :] = jnp.where(lane < row, rows[q], jnp.where(lane == row, scales[q], 0.0))


def factor_kernel(width, me_ref, *refs):
    *pieces, u_out, mine_out, quad_ref, tok_ref, sum_ref, len_ref, p_ref, f_ref, u_ref, s_ref, d_ref, m_ref, sems = refs
    n_rep = len(pieces)
    docs = p_ref.shape[0]
    rows = docs // n_rep
    tokens = p_ref.shape[1]
    me = me_ref[0]
    for d in range(n_rep):
        tok_ref[me ^ d] = pieces[d][...]
    sum_ref[...] = jnp.zeros_like(sum_ref)
    len_ref[...] = jnp.zeros_like(len_ref)
    side = (tok_ref.shape[1] - 16) // 2
    doc = lax.broadcasted_iota(jnp.int32, (docs, tokens), 0).astype(jnp.float32)
    ones = jnp.ones((16, tokens), jnp.bfloat16)
    tall = 8 * side

    def add_tokens(r, last):
        left = tok_ref[r, 0:side, :].astype(jnp.float32)
        right = tok_ref[r, side : 2 * side, :].astype(jnp.float32)
        coded = tok_ref[r, 2 * side :, :].astype(jnp.float32)
        target = coded[0:1, :] * 32.0 + coded[1:2, :]
        target = jnp.where(target < 0.0, last, target)
        p_ref[...] = jnp.where(doc == target, 1.0, 0.0).astype(jnp.bfloat16)
        len_ref[...] += dot_n(ones, p_ref[...])
        for q in range(0, side, 8):
            outer = jnp.concatenate(
                [jnp.broadcast_to(left[i : i + 1, :], right.shape) * right for i in range(q, q + 8)], 0
            )
            high = outer.astype(jnp.bfloat16)
            low = (outer - high.astype(jnp.float32)).astype(jnp.bfloat16)
            sum_ref[q * side : q * side + tall, :] += dot_n(high, p_ref[...]) + dot_n(low, p_ref[...])
        return target[:, tokens - 1 : tokens]

    lax.fori_loop(0, n_rep, add_tokens, jnp.zeros((1, 1), jnp.float32))
    scale = lax.rsqrt(jnp.maximum(len_ref[0:1, :], 1.0))
    f_ref[...] = (sum_ref[...] * scale).astype(jnp.bfloat16)
    row = lax.broadcasted_iota(jnp.int32, (docs, BLK), 0)
    slot = lax.broadcasted_iota(jnp.int32, (docs, BLK), 1)
    pick = jnp.where((row == me * rows + slot) & (slot < rows), 1.0, 0.0).astype(jnp.bfloat16)
    row = lax.broadcasted_iota(jnp.int32, (rows, docs), 0)
    slot = lax.broadcasted_iota(jnp.int32, (rows, docs), 1)
    pick_t = jnp.where(slot == me * rows + row, 1.0, 0.0).astype(jnp.bfloat16)
    mine_out[...] = dot_n(pick_t, f_ref[...]).astype(jnp.bfloat16)
    eye = jnp.where(
        lax.broadcasted_iota(jnp.int32, (PAN, PAN), 0) == lax.broadcasted_iota(jnp.int32, (PAN, PAN), 1),
        DAMPING,
        0.0,
    )

    def start_panel(k):
        a, c = PAN * k, PAN * k + PAN
        gram = dot_n(f_ref[a:c, :], f_ref[a:, :]) * (1.0 / docs)
        own = dot(f_ref[a:c, :], pick, None)
        if k:
            done = u_ref[0:a, a:c]
            gram = gram - dot_t(done, u_ref[0:a, a:width])
            own = own - dot_t(done, u_ref[0:a, width:])
            u_ref[a:c, 0:a] = jnp.zeros((PAN, a), jnp.float32)
        u_ref[a + BLK : c, a : a + BLK] = jnp.zeros((BLK, BLK), jnp.float32)
        s_ref[:, a:c] = gram[:, 0:PAN] + eye
        if c < width:
            s_ref[:, c:width] = gram[:, PAN:]
        s_ref[:, width:] = own
        d_ref[...] = s_ref[0:BLK, a : a + BLK]

    def first_half(k):
        a, b, c = PAN * k, PAN * k + BLK, PAN * k + PAN
        upper = dot(m_ref[...], s_ref[0:BLK, b:])
        u_ref[a:b, b:] = upper
        update = dot_t(upper[:, 0:BLK], upper)
        d_ref[...] = s_ref[BLK:, b:c] - update[:, 0:BLK]
        s_ref[BLK:, c:] = s_ref[BLK:, c:] - update[:, BLK:]

    def panel_copy(k):
        at = pl.ds(PAN * k, PAN)
        return pltpu.make_async_copy(u_ref.at[at, 0:width], u_out.at[at, :], sems.at[k])

    def second_half(k):
        b, c = PAN * k + BLK, PAN * k + PAN
        u_ref[b:c, c:] = dot(m_ref[...], s_ref[BLK:, c:])
        panel_copy(k).start()
        if c < width:
            start_panel(k + 1)

    start_panel(0)

    def block(m, carry):
        at = pl.ds(pl.multiple_of(m * BLK, BLK), BLK)
        factor_block(d_ref, u_ref.at[at, at], m_ref)
        for i in range(width // BLK):

            @pl.when(m == i)
            def _():
                (second_half if i % 2 else first_half)(i // 2)

        return carry

    lax.fori_loop(0, width // BLK, block, 0)
    solved = u_ref[:, width:]
    quad = jnp.sum(solved * solved, axis=0, keepdims=True) * (1.0 / width)
    quad_ref[...] = quad
    for k in range(width // PAN):
        panel_copy(k).wait()


def factor_and_solve(pieces, replica):
    n_rep = len(pieces)
    height, tokens = pieces[0].shape
    width = ((height - 16) // 2) ** 2
    docs = n_rep * BAL
    return pl.pallas_call(
        functools.partial(factor_kernel, width),
        out_shape=[
            jax.ShapeDtypeStruct((width, width), jnp.float32),
            jax.ShapeDtypeStruct((BAL, width), jnp.bfloat16),
            jax.ShapeDtypeStruct((1, BLK), jnp.float32),
        ],
        in_specs=[pl.BlockSpec(memory_space=pltpu.SMEM)] + [VMEM] * n_rep,
        out_specs=[pl.BlockSpec(memory_space=pl.ANY), VMEM, VMEM],
        scratch_shapes=[
            pltpu.VMEM((n_rep, height, tokens), jnp.bfloat16),
            pltpu.VMEM((width, docs), jnp.float32),
            pltpu.VMEM((16, docs), jnp.float32),
            pltpu.VMEM((docs, tokens), jnp.bfloat16),
            pltpu.VMEM((width, docs), jnp.bfloat16),
            pltpu.VMEM((width, width + BLK), jnp.float32),
            pltpu.VMEM((PAN, width + BLK), jnp.float32),
            pltpu.VMEM((BLK, BLK), jnp.float32),
            pltpu.VMEM((BLK, BLK), jnp.float32),
            pltpu.SemaphoreType.DMA((width // PAN,)),
        ],
        compiler_params=pltpu.CompilerParams(vmem_limit_bytes=48 * 1024 * 1024),
        name="factor",
    )(jnp.reshape(replica, (1,)).astype(jnp.int32), *pieces)


def on_device(activations, output_grads, in_projection, out_projection, segment_ids, move_list):
    tokens = project(
        activations[0], output_grads[0], in_projection[0], out_projection[0], segment_ids, move_list
    )
    upper, mine, quad = factor_and_solve(gathered(tokens, "rep"), lax.axis_index("rep"))
    layers = [quad] + [swapped(quad, "layer", d) for d in range(1, lax.axis_size("layer"))]
    while len(layers) > 1:
        layers = [layers[i] + layers[i + 1] for i in range(0, len(layers), 2)]
    return (upper[None], mine[None], layers[0][0, :BAL])


def solution(mesh):
    placed = (
        P("layer", "rep", None),
        P("layer", "rep", None),
        P("layer", None, None),
        P("layer", None, None),
        P("rep"),
        P("rep"),
    )
    return jax.shard_map(
        on_device,
        mesh=mesh,
        in_specs=placed,
        out_specs=(P("layer", None, None), P("layer", "rep", None), P("rep")),
        check_vma=False,
    )
```

```python
import functools

import jax
import jax.numpy as jnp
from jax import lax
from jax.experimental import pallas as pl
from jax.experimental.pallas import tpu as pltpu
from jax.sharding import PartitionSpec as P

BAL = 32
DAMPING = 0.05
BLK = 128
PAN = 256
SUP = 64
EXACT = lax.Precision.HIGHEST
VMEM = pl.BlockSpec(memory_space=pltpu.VMEM)
FAR = pl.BlockSpec(memory_space=pltpu.HBM)


def swapped(block, axis, distance):
    devices = range(lax.axis_size(axis))
    return lax.ppermute(block, axis, [(i, i ^ distance) for i in devices])


def gathered(block, axis):
    even = [swapped(block, axis, d) for d in range(2, lax.axis_size(axis), 2)]
    pieces = [block, swapped(block, axis, 1)]
    for piece in even:
        pieces += [piece, swapped(piece, axis, 1)]
    return pieces


def lane_of(v, j):
    return jnp.take_along_axis(v, jnp.full(v.shape, j, jnp.int32), axis=1)


def row_of(v, s):
    return jnp.broadcast_to(v[s : s + 1, :], v.shape)


def dot(a, b, precision=EXACT):
    return jnp.dot(a, b, precision=precision, preferred_element_type=jnp.float32)


def dot_t(a, b, precision=EXACT):
    return lax.dot_general(
        a, b, (((0,), (0,)), ((), ())), precision=precision, preferred_element_type=jnp.float32
    )


def dot_n(a, b):
    return lax.dot_general(a, b, (((1,), (1,)), ((), ())), preferred_element_type=jnp.float32)


def project_kernel(acts, grads, w_in, w_out, segments, moves, out, a_ref, g_ref, wi_ref, wo_ref, seg_ref, move_ref, sems):
    tokens, depth = a_ref.shape
    parts = sems.shape[0] // 2 - 2
    deep = depth // parts
    width = w_in.shape[0]
    small = [
        pltpu.make_async_copy(segments, seg_ref, sems.at[2 * parts]),
        pltpu.make_async_copy(moves, move_ref, sems.at[2 * parts + 1]),
    ]
    weights = [
        pltpu.make_async_copy(w_in, wi_ref, sems.at[2 * parts + 2]),
        pltpu.make_async_copy(w_out, wo_ref, sems.at[2 * parts + 3]),
    ]
    copies = []
    for c in range(parts):
        at = pl.ds(c * deep, deep)
        copies += [
            pltpu.make_async_copy(acts.at[:, at], a_ref.at[:, at], sems.at[2 * c]),
            pltpu.make_async_copy(grads.at[:, at], g_ref.at[:, at], sems.at[2 * c + 1]),
        ]
    for copy in [*small, *weights, *copies]:
        copy.start()
    for copy in small:
        copy.wait()
    slots = moves.shape[1]
    slot = lax.broadcasted_iota(jnp.int32, (slots, slots), 0)
    other = lax.broadcasted_iota(jnp.int32, (slots, slots), 1)
    column = jnp.sum(jnp.where(slot == other, move_ref[...], 0), axis=1, keepdims=True)
    segment = seg_ref[...]
    slot = lax.broadcasted_iota(jnp.int32, (slots, tokens), 0)
    target = jnp.sum(jnp.where(slot == segment, column, 0), axis=0, keepdims=True)
    target = jnp.where(segment < 0, -1, target)
    line = lax.broadcasted_iota(jnp.int32, (16, tokens), 0)
    coded = jnp.where(line == 0, target >> 5, jnp.where(line == 1, target & 31, 0))
    out[2 * width :, :] = coded.astype(jnp.float32).astype(jnp.bfloat16)
    for copy in weights:
        copy.wait()
    left = right = jnp.zeros((tokens, width), jnp.float32)
    for c in range(parts):
        at = slice(c * deep, c * deep + deep)
        copies[2 * c].wait()
        copies[2 * c + 1].wait()
        left = left + dot_n(a_ref[:, at], wi_ref[:, at])
        right = right + dot_n(g_ref[:, at], wo_ref[:, at])
    out[0:width, :] = left.T.astype(jnp.bfloat16)
    out[width : 2 * width, :] = right.T.astype(jnp.bfloat16)


def project(activations, output_grads, in_projection, out_projection, segment_ids, move_list):
    tokens, depth = activations.shape
    width = in_projection.shape[0]
    slots = move_list.shape[0]
    parts = depth // 512
    return pl.pallas_call(
        project_kernel,
        out_shape=jax.ShapeDtypeStruct((2 * width + 16, tokens), jnp.bfloat16),
        in_specs=[FAR] * 6,
        out_specs=VMEM,
        scratch_shapes=[
            pltpu.VMEM((tokens, depth), jnp.bfloat16),
            pltpu.VMEM((tokens, depth), jnp.bfloat16),
            pltpu.VMEM((width, depth), jnp.bfloat16),
            pltpu.VMEM((width, depth), jnp.bfloat16),
            pltpu.VMEM((1, tokens), jnp.int32),
            pltpu.VMEM((1, slots), jnp.int32),
            pltpu.SemaphoreType.DMA((2 * parts + 4,)),
        ],
        compiler_params=pltpu.CompilerParams(vmem_limit_bytes=58 * 1024 * 1024),
        name="project",
    )(
        activations,
        output_grads,
        in_projection,
        out_projection,
        segment_ids.reshape(1, tokens),
        move_list.reshape(1, slots),
    )


def eliminate(x, first):
    lane = lax.broadcasted_iota(jnp.int32, (8, BLK), 1)
    sub = lax.broadcasted_iota(jnp.int32, (8, BLK), 0)
    x, count = list(x), len(x)
    scales = [None] * count
    spread = lambda group, lo: [lane_of(group, lo + c) for c in range(8)]
    cols = spread(x[0], first)
    for t in range(count):
        lo = first + 8 * t
        work = x[t]
        more = t + 1 < count
        if more:
            below = [spread(x[i], lo) for i in range(t + 1, count)]
            side = spread(x[t], lo + 8)
            ahead = spread(x[t + 1], lo + 8)
            factor = list(below[0])
        kept, pivots = work, jnp.ones((8, BLK), jnp.float32)
        for c in range(8):
            hit, at = sub == c, lane == lo + c
            pivot = row_of(cols[c], c)
            inv = 1.0 / pivot
            kept = jnp.where(hit, work, kept)
            pivots = jnp.where(hit, pivot, pivots)
            row = jnp.where(at, 1.0, row_of(work, c)) * inv
            work = jnp.where(hit, row, jnp.where(at, 0.0, work) - cols[c] * row)
            under = jnp.where(sub > c, cols[c], 0.0)
            for k in range(c + 1, 8):
                raw = row_of(cols[k], c)
                weight = raw * inv
                if k == c + 1:
                    new = cols[k] - (cols[c] * raw) * inv
                else:
                    new = cols[k] - cols[c] * weight
                cols[k] = jnp.where(hit, weight, new)
                if more:
                    factor[k] = factor[k] - factor[c] * weight
            if more:
                for k in range(8):
                    raw = row_of(side[k], c)
                    weight = raw * inv
                    if c < 7:
                        side[k] = side[k] - under * weight
                    ahead[k] = ahead[k] - factor[c] * weight
        if more:
            inside = (lane >= lo) & (lane < lo + 8)
            rows = [row_of(work, c) for c in range(8)]
            for i in range(t + 1, count):
                terms = [below[i - t - 1][c] * rows[c] for c in range(8)]
                while len(terms) > 1:
                    terms = [terms[m] + terms[m + 1] for m in range(0, len(terms), 2)]
                x[i] = jnp.where(inside, 0.0, x[i]) - terms[0]
            cols = ahead
        scales[t] = lax.rsqrt(pivots)
        x[t] = kept * scales[t]
    return x, scales


def factor_block(d_ref, u_ref, m_ref):
    lane = lax.broadcasted_iota(jnp.int32, (8, BLK), 1)
    sub = lax.broadcasted_iota(jnp.int32, (8, BLK), 0)
    tall_row = lax.broadcasted_iota(jnp.int32, (SUP, BLK), 0)
    tall_lane = lax.broadcasted_iota(jnp.int32, (SUP, BLK), 1)
    groups, n = BLK // 8, SUP // 8
    x = [d_ref[8 * i : 8 * i + 8, :] for i in range(groups)]
    for h in range(0, groups, n):
        a, b = 8 * h, 8 * (h + n)
        rows, scales = eliminate(x[h : h + n], a)
        if b < BLK:
            block, scale = jnp.concatenate(rows, 0), jnp.concatenate(scales, 0)
            row = tall_row + a
            right = jnp.where(
                (tall_lane > row) & (tall_lane < b), 0.0, jnp.where(tall_lane == row, scale, block)
            )
            update = dot_t(block, right)
            for i in range(h + n, groups):
                x[i] = jnp.where((lane >= a) & (lane < b), 0.0, x[i]) - update[8 * i : 8 * i + 8, :]
        for q in range(n):
            row = a + 8 * q + sub
            at = slice(a + 8 * q, a + 8 * q + 8)
            u_ref[at, :] = jnp.where(lane >= row, rows[q], 0.0)
            m_ref[at, :] = jnp.where(lane < row, rows[q], jnp.where(lane == row, scales[q], 0.0))


def factor_kernel(width, me_ref, *refs):
    *pieces, u_out, mine_out, quad_ref, tok_ref, sum_ref, len_ref, p_ref, f_ref, u_ref, s_ref, d_ref, m_ref, sems = refs
    n_rep = len(pieces)
    docs = p_ref.shape[0]
    rows = docs // n_rep
    tokens = p_ref.shape[1] // 4
    me = me_ref[0]
    for d in range(n_rep):
        tok_ref[me ^ d] = pieces[d][...]
    sum_ref[...] = jnp.zeros_like(sum_ref)
    len_ref[...] = jnp.zeros_like(len_ref)
    side = (tok_ref.shape[1] - 16) // 2
    doc = lax.broadcasted_iota(jnp.int32, (docs, tokens), 0).astype(jnp.float32)
    ones = jnp.ones((16, 2 * tokens), jnp.bfloat16)
    tall = 8 * side

    def add_tokens(pair, last):
        for h in range(2):
            coded = tok_ref[2 * pair + h, 2 * side :, :].astype(jnp.float32)
            target = coded[0:1, :] * 32.0 + coded[1:2, :]
            target = jnp.where(target < 0.0, last, target)
            last = target[:, tokens - 1 : tokens]
            member = jnp.where(doc == target, 1.0, 0.0).astype(jnp.bfloat16)
            p_ref[:, h * tokens : (h + 1) * tokens] = member
            p_ref[:, (h + 2) * tokens : (h + 3) * tokens] = member
        len_ref[...] += dot_n(ones, p_ref[:, 0 : 2 * tokens])
        lefts = [tok_ref[2 * pair + h, 0:side, :].astype(jnp.float32) for h in range(2)]
        rights = [tok_ref[2 * pair + h, side : 2 * side, :].astype(jnp.float32) for h in range(2)]
        for q in range(0, side, 8):
            highs, lows = [], []
            for h in range(2):
                left, right = lefts[h], rights[h]
                outer = jnp.concatenate(
                    [jnp.broadcast_to(left[i : i + 1, :], right.shape) * right for i in range(q, q + 8)], 0
                )
                highs.append(outer.astype(jnp.bfloat16))
                lows.append((outer - highs[h].astype(jnp.float32)).astype(jnp.bfloat16))
            parts = jnp.concatenate(highs + lows, 1)
            sum_ref[q * side : q * side + tall, :] += dot_n(parts, p_ref[...])
        return last

    lax.fori_loop(0, n_rep // 2, add_tokens, jnp.zeros((1, 1), jnp.float32))
    scale = lax.rsqrt(jnp.maximum(len_ref[0:1, :], 1.0))
    f_ref[...] = (sum_ref[...] * scale).astype(jnp.bfloat16)
    row = lax.broadcasted_iota(jnp.int32, (docs, BLK), 0)
    slot = lax.broadcasted_iota(jnp.int32, (docs, BLK), 1)
    pick = jnp.where((row == me * rows + slot) & (slot < rows), 1.0, 0.0).astype(jnp.bfloat16)
    row = lax.broadcasted_iota(jnp.int32, (rows, docs), 0)
    slot = lax.broadcasted_iota(jnp.int32, (rows, docs), 1)
    pick_t = jnp.where(slot == me * rows + row, 1.0, 0.0).astype(jnp.bfloat16)
    mine_out[...] = dot_n(pick_t, f_ref[...]).astype(jnp.bfloat16)
    eye = jnp.where(
        lax.broadcasted_iota(jnp.int32, (PAN, PAN), 0) == lax.broadcasted_iota(jnp.int32, (PAN, PAN), 1),
        DAMPING,
        0.0,
    )

    def start_panel(k):
        a, c = PAN * k, PAN * k + PAN
        gram = dot_n(f_ref[a:c, :], f_ref[a:, :]) * (1.0 / docs)
        own = dot(f_ref[a:c, :], pick, None)
        if k:
            done = u_ref[0:a, a:c]
            gram = gram - dot_t(done, u_ref[0:a, a:width])
            own = own - dot_t(done, u_ref[0:a, width:])
            u_ref[a:c, 0:a] = jnp.zeros((PAN, a), jnp.float32)
        u_ref[a + BLK : c, a : a + BLK] = jnp.zeros((BLK, BLK), jnp.float32)
        s_ref[:, a:c] = gram[:, 0:PAN] + eye
        if c < width:
            s_ref[:, c:width] = gram[:, PAN:]
        s_ref[:, width:] = own
        d_ref[...] = s_ref[0:BLK, a : a + BLK]

    def first_half(k):
        a, b, c = PAN * k, PAN * k + BLK, PAN * k + PAN
        upper = dot(m_ref[...], s_ref[0:BLK, b:])
        u_ref[a:b, b:] = upper
        update = dot_t(upper[:, 0:BLK], upper)
        d_ref[...] = s_ref[BLK:, b:c] - update[:, 0:BLK]
        s_ref[BLK:, c:] = s_ref[BLK:, c:] - update[:, BLK:]

    def panel_copy(k):
        at = pl.ds(PAN * k, PAN)
        return pltpu.make_async_copy(u_ref.at[at, 0:width], u_out.at[at, :], sems.at[k])

    def second_half(k):
        b, c = PAN * k + BLK, PAN * k + PAN
        u_ref[b:c, c:] = dot(m_ref[...], s_ref[BLK:, c:])
        panel_copy(k).start()
        if c < width:
            start_panel(k + 1)

    start_panel(0)

    def block(m, carry):
        at = pl.ds(pl.multiple_of(m * BLK, BLK), BLK)
        factor_block(d_ref, u_ref.at[at, at], m_ref)
        for i in range(width // BLK):

            @pl.when(m == i)
            def _():
                (second_half if i % 2 else first_half)(i // 2)

        return carry

    lax.fori_loop(0, width // BLK, block, 0)
    solved = u_ref[:, width:]
    quad = jnp.sum(solved * solved, axis=0, keepdims=True) * (1.0 / width)
    quad_ref[...] = quad
    for k in range(width // PAN):
        panel_copy(k).wait()


def factor_and_solve(pieces, replica):
    n_rep = len(pieces)
    height, tokens = pieces[0].shape
    width = ((height - 16) // 2) ** 2
    docs = n_rep * BAL
    return pl.pallas_call(
        functools.partial(factor_kernel, width),
        out_shape=[
            jax.ShapeDtypeStruct((width, width), jnp.float32),
            jax.ShapeDtypeStruct((BAL, width), jnp.bfloat16),
            jax.ShapeDtypeStruct((1, BLK), jnp.float32),
        ],
        in_specs=[pl.BlockSpec(memory_space=pltpu.SMEM)] + [VMEM] * n_rep,
        out_specs=[pl.BlockSpec(memory_space=pl.ANY), VMEM, VMEM],
        scratch_shapes=[
            pltpu.VMEM((n_rep, height, tokens), jnp.bfloat16),
            pltpu.VMEM((width, docs), jnp.float32),
            pltpu.VMEM((16, docs), jnp.float32),
            pltpu.VMEM((docs, 4 * tokens), jnp.bfloat16),
            pltpu.VMEM((width, docs), jnp.bfloat16),
            pltpu.VMEM((width, width + BLK), jnp.float32),
            pltpu.VMEM((PAN, width + BLK), jnp.float32),
            pltpu.VMEM((BLK, BLK), jnp.float32),
            pltpu.VMEM((BLK, BLK), jnp.float32),
            pltpu.SemaphoreType.DMA((width // PAN,)),
        ],
        compiler_params=pltpu.CompilerParams(vmem_limit_bytes=48 * 1024 * 1024),
        name="factor",
    )(jnp.reshape(replica, (1,)).astype(jnp.int32), *pieces)


def on_device(activations, output_grads, in_projection, out_projection, segment_ids, move_list):
    tokens = project(
        activations[0], output_grads[0], in_projection[0], out_projection[0], segment_ids, move_list
    )
    upper, mine, quad = factor_and_solve(gathered(tokens, "rep"), lax.axis_index("rep"))
    layers = [quad] + [swapped(quad, "layer", d) for d in range(1, lax.axis_size("layer"))]
    while len(layers) > 1:
        layers = [layers[i] + layers[i + 1] for i in range(0, len(layers), 2)]
    return (upper[None], mine[None], layers[0][0, :BAL])


def solution(mesh):
    placed = (
        P("layer", "rep", None),
        P("layer", "rep", None),
        P("layer", None, None),
        P("layer", None, None),
        P("rep"),
        P("rep"),
    )
    return jax.shard_map(
        on_device,
        mesh=mesh,
        in_specs=placed,
        out_specs=(P("layer", None, None), P("layer", "rep", None), P("rep")),
        check_vma=False,
    )
```

```python
import functools

import jax
import jax.numpy as jnp
from jax import lax
from jax.experimental import pallas as pl
from jax.experimental.pallas import tpu as pltpu
from jax.sharding import PartitionSpec as P

BAL = 32
DAMPING = 0.05
BLK = 128
PAN = 256
SUP = 64
EXACT = lax.Precision.HIGHEST
VMEM = pl.BlockSpec(memory_space=pltpu.VMEM)
FAR = pl.BlockSpec(memory_space=pltpu.HBM)


def swapped(block, axis, distance):
    devices = range(lax.axis_size(axis))
    return lax.ppermute(block, axis, [(i, i ^ distance) for i in devices])


def gathered(block, axis):
    even = [swapped(block, axis, d) for d in range(2, lax.axis_size(axis), 2)]
    pieces = [block, swapped(block, axis, 1)]
    for piece in even:
        pieces += [piece, swapped(piece, axis, 1)]
    return pieces


def lane_of(v, j):
    return jnp.take_along_axis(v, jnp.full(v.shape, j, jnp.int32), axis=1)


def row_of(v, s):
    return jnp.broadcast_to(v[s : s + 1, :], v.shape)


def dot_t(a, b):
    return lax.dot_general(
        a, b, (((0,), (0,)), ((), ())), precision=EXACT, preferred_element_type=jnp.float32
    )


def split(x):
    high = x.astype(jnp.bfloat16)
    rest = x - high.astype(jnp.float32)
    middle = rest.astype(jnp.bfloat16)
    return high, middle, (rest - middle.astype(jnp.float32)).astype(jnp.bfloat16)


def dot_parts(a, b, dim_a, dim_b=0):
    left = jnp.concatenate([a[2], a[1], a[0], a[1], a[0], a[0]], dim_a)
    right = jnp.concatenate([b[0], b[1], b[2], b[0], b[1], b[0]], dim_b)
    dims = (((dim_a,), (dim_b,)), ((), ()))
    return lax.dot_general(left, right, dims, preferred_element_type=jnp.float32)


def dot_n(a, b):
    return lax.dot_general(a, b, (((1,), (1,)), ((), ())), preferred_element_type=jnp.float32)


def project_kernel(acts, grads, w_in, w_out, segments, moves, out, a_ref, g_ref, wi_ref, wo_ref, seg_ref, move_ref, sems):
    tokens, depth = a_ref.shape
    parts = sems.shape[0] // 2 - 2
    deep = depth // parts
    width = w_in.shape[0]
    small = [
        pltpu.make_async_copy(segments, seg_ref, sems.at[2 * parts]),
        pltpu.make_async_copy(moves, move_ref, sems.at[2 * parts + 1]),
    ]
    weights = [
        pltpu.make_async_copy(w_in, wi_ref, sems.at[2 * parts + 2]),
        pltpu.make_async_copy(w_out, wo_ref, sems.at[2 * parts + 3]),
    ]
    copies = []
    for c in range(parts):
        at = pl.ds(c * deep, deep)
        copies += [
            pltpu.make_async_copy(acts.at[:, at], a_ref.at[:, at], sems.at[2 * c]),
            pltpu.make_async_copy(grads.at[:, at], g_ref.at[:, at], sems.at[2 * c + 1]),
        ]
    for copy in [*small, *weights, *copies]:
        copy.start()
    for copy in small:
        copy.wait()
    slots = moves.shape[1]
    slot = lax.broadcasted_iota(jnp.int32, (slots, slots), 0)
    other = lax.broadcasted_iota(jnp.int32, (slots, slots), 1)
    column = jnp.sum(jnp.where(slot == other, move_ref[...], 0), axis=1, keepdims=True)
    segment = seg_ref[...]
    slot = lax.broadcasted_iota(jnp.int32, (slots, tokens), 0)
    target = jnp.sum(jnp.where(slot == segment, column, 0), axis=0, keepdims=True)
    target = jnp.where(segment < 0, -1, target)
    line = lax.broadcasted_iota(jnp.int32, (16, tokens), 0)
    coded = jnp.where(line == 0, target >> 5, jnp.where(line == 1, target & 31, 0))
    out[2 * width :, :] = coded.astype(jnp.float32).astype(jnp.bfloat16)
    for copy in weights:
        copy.wait()
    left = right = jnp.zeros((tokens, width), jnp.float32)
    for c in range(parts):
        at = slice(c * deep, c * deep + deep)
        copies[2 * c].wait()
        copies[2 * c + 1].wait()
        left = left + dot_n(a_ref[:, at], wi_ref[:, at])
        right = right + dot_n(g_ref[:, at], wo_ref[:, at])
    out[0:width, :] = left.T.astype(jnp.bfloat16)
    out[width : 2 * width, :] = right.T.astype(jnp.bfloat16)


def project(activations, output_grads, in_projection, out_projection, segment_ids, move_list):
    tokens, depth = activations.shape
    width = in_projection.shape[0]
    slots = move_list.shape[0]
    parts = depth // 512
    return pl.pallas_call(
        project_kernel,
        out_shape=jax.ShapeDtypeStruct((2 * width + 16, tokens), jnp.bfloat16),
        in_specs=[FAR] * 6,
        out_specs=VMEM,
        scratch_shapes=[
            pltpu.VMEM((tokens, depth), jnp.bfloat16),
            pltpu.VMEM((tokens, depth), jnp.bfloat16),
            pltpu.VMEM((width, depth), jnp.bfloat16),
            pltpu.VMEM((width, depth), jnp.bfloat16),
            pltpu.VMEM((1, tokens), jnp.int32),
            pltpu.VMEM((1, slots), jnp.int32),
            pltpu.SemaphoreType.DMA((2 * parts + 4,)),
        ],
        compiler_params=pltpu.CompilerParams(vmem_limit_bytes=58 * 1024 * 1024),
        name="project",
    )(
        activations,
        output_grads,
        in_projection,
        out_projection,
        segment_ids.reshape(1, tokens),
        move_list.reshape(1, slots),
    )


def eliminate(x, first):
    lane = lax.broadcasted_iota(jnp.int32, (8, BLK), 1)
    sub = lax.broadcasted_iota(jnp.int32, (8, BLK), 0)
    x, count = list(x), len(x)
    scales = [None] * count
    spread = lambda group, lo: [lane_of(group, lo + c) for c in range(8)]
    cols = spread(x[0], first)
    pivot = row_of(cols[0], 0)
    for t in range(count):
        lo = first + 8 * t
        work = x[t]
        more = t + 1 < count
        if more:
            below = [spread(x[i], lo) for i in range(t + 1, count)]
            ahead = spread(x[t + 1], lo + 8)
            factor = list(below[0])
        kept, pivots = work, jnp.ones((8, BLK), jnp.float32)
        for c in range(8):
            hit, at = sub == c, lane == lo + c
            inv = 1.0 / pivot
            kept = jnp.where(hit, work, kept)
            pivots = jnp.where(hit, pivot, pivots)
            other = jnp.where(hit, 0.0, cols[c])
            scaled = other * inv
            raws = {k: row_of(cols[c], k) for k in range(c + 1, 8)}
            if c < 7:
                pivot = row_of(cols[c + 1], c + 1) - (raws[c + 1] * raws[c + 1]) * inv
            elif more:
                edge = row_of(factor[7], 0)
                pivot = row_of(ahead[0], 0) - (edge * edge) * inv
            row = jnp.where(at, 1.0, row_of(work, c))
            work = jnp.where(at, jnp.where(hit, 1.0, 0.0), work) - scaled * row
            for k in range(c + 1, 8):
                cols[k] = cols[k] - scaled * raws[k]
            if more:
                part = factor[c] * inv
                for k in range(c + 1, 8):
                    factor[k] = factor[k] - part * raws[k]
                for k in range(8):
                    ahead[k] = ahead[k] - part * row_of(factor[c], k)
        work = work * (1.0 / pivots)
        if more:
            inside = (lane >= lo) & (lane < lo + 8)
            rows = [row_of(work, c) for c in range(8)]
            for i in range(t + 1, count):
                terms = [below[i - t - 1][c] * rows[c] for c in range(8)]
                while len(terms) > 1:
                    terms = [terms[m] + terms[m + 1] for m in range(0, len(terms), 2)]
                x[i] = jnp.where(inside, 0.0, x[i]) - terms[0]
            cols = ahead
        scales[t] = lax.rsqrt(pivots)
        x[t] = kept * scales[t]
    return x, scales


def factor_block(d_ref, u_ref, m_ref):
    lane = lax.broadcasted_iota(jnp.int32, (8, BLK), 1)
    sub = lax.broadcasted_iota(jnp.int32, (8, BLK), 0)
    tall_row = lax.broadcasted_iota(jnp.int32, (SUP, BLK), 0)
    tall_lane = lax.broadcasted_iota(jnp.int32, (SUP, BLK), 1)
    groups, n = BLK // 8, SUP // 8
    x = [d_ref[8 * i : 8 * i + 8, :] for i in range(groups)]
    for h in range(0, groups, n):
        a, b = 8 * h, 8 * (h + n)
        rows, scales = eliminate(x[h : h + n], a)
        if b < BLK:
            block, scale = jnp.concatenate(rows, 0), jnp.concatenate(scales, 0)
            row = tall_row + a
            right = jnp.where(
                (tall_lane > row) & (tall_lane < b), 0.0, jnp.where(tall_lane == row, scale, block)
            )
            update = dot_t(block, right)
            for i in range(h + n, groups):
                x[i] = jnp.where((lane >= a) & (lane < b), 0.0, x[i]) - update[8 * i : 8 * i + 8, :]
        for q in range(n):
            row = a + 8 * q + sub
            at = slice(a + 8 * q, a + 8 * q + 8)
            u_ref[at, :] = jnp.where(lane >= row, rows[q], 0.0)
            m_ref[at, :] = jnp.where(lane < row, rows[q], jnp.where(lane == row, scales[q], 0.0))


def factor_kernel(width, me_ref, *refs):
    *pieces, u_out, mine_out, quad_ref, tok_ref, sum_ref, len_ref, p_ref, f_ref, u_ref, u3_ref, s_ref, y_ref, own_ref, d_ref, m_ref, sems = refs
    n_rep = len(pieces)
    docs = p_ref.shape[0]
    rows = docs // n_rep
    tokens = p_ref.shape[1] // 4
    me = me_ref[0]
    for d in range(n_rep):
        tok_ref[me ^ d] = pieces[d][...]
    sum_ref[...] = jnp.zeros_like(sum_ref)
    len_ref[...] = jnp.zeros_like(len_ref)
    side = (tok_ref.shape[1] - 16) // 2
    doc = lax.broadcasted_iota(jnp.int32, (docs, tokens), 0).astype(jnp.float32)
    ones = jnp.ones((16, 2 * tokens), jnp.bfloat16)
    tall = 8 * side

    def add_tokens(pair, last):
        for h in range(2):
            coded = tok_ref[2 * pair + h, 2 * side :, :].astype(jnp.float32)
            target = coded[0:1, :] * 32.0 + coded[1:2, :]
            target = jnp.where(target < 0.0, last, target)
            last = target[:, tokens - 1 : tokens]
            member = jnp.where(doc == target, 1.0, 0.0).astype(jnp.bfloat16)
            p_ref[:, h * tokens : (h + 1) * tokens] = member
            p_ref[:, (h + 2) * tokens : (h + 3) * tokens] = member
        len_ref[...] += dot_n(ones, p_ref[:, 0 : 2 * tokens])
        lefts = [tok_ref[2 * pair + h, 0:side, :].astype(jnp.float32) for h in range(2)]
        rights = [tok_ref[2 * pair + h, side : 2 * side, :].astype(jnp.float32) for h in range(2)]
        for q in range(0, side, 8):
            highs, lows = [], []
            for h in range(2):
                left, right = lefts[h], rights[h]
                outer = jnp.concatenate(
                    [jnp.broadcast_to(left[i : i + 1, :], right.shape) * right for i in range(q, q + 8)], 0
                )
                highs.append(outer.astype(jnp.bfloat16))
                lows.append((outer - highs[h].astype(jnp.float32)).astype(jnp.bfloat16))
            parts = jnp.concatenate(highs + lows, 1)
            sum_ref[q * side : q * side + tall, :] += dot_n(parts, p_ref[...])
        return last

    lax.fori_loop(0, n_rep // 2, add_tokens, jnp.zeros((1, 1), jnp.float32))
    scale = lax.rsqrt(jnp.maximum(len_ref[0:1, :], 1.0))
    f_ref[...] = (sum_ref[...] * scale).astype(jnp.bfloat16)
    row = lax.broadcasted_iota(jnp.int32, (rows, docs), 0)
    slot = lax.broadcasted_iota(jnp.int32, (rows, docs), 1)
    pick_t = jnp.where(slot == me * rows + row, 1.0, 0.0).astype(jnp.bfloat16)
    mine_out[...] = dot_n(pick_t, f_ref[...]).astype(jnp.bfloat16)
    eye = jnp.where(
        lax.broadcasted_iota(jnp.int32, (PAN, PAN), 0) == lax.broadcasted_iota(jnp.int32, (PAN, PAN), 1),
        DAMPING,
        0.0,
    )

    def start_panel(k):
        a, c = PAN * k, PAN * k + PAN
        s_ref[:, a:] = dot_n(f_ref[a:c, :], f_ref[a:, :]) * (1.0 / docs)
        s_ref[:, a:c] = s_ref[:, a:c] + eye
        own = mine_out[:, a:c].astype(jnp.float32)
        if k:
            done = [u3_ref[p, 0:a, a:c] for p in range(3)]
            s_ref[:, a:] = s_ref[:, a:] - dot_parts(done, [u3_ref[p, 0:a, a:] for p in range(3)], 0)
            own = own - dot_parts(split(y_ref[:, 0:a]), done, 1)
            u_ref[a:c, 0:a] = jnp.zeros((PAN, a), jnp.float32)
        own_ref[...] = own
        u_ref[a + BLK : c, a : a + BLK] = jnp.zeros((BLK, BLK), jnp.float32)
        d_ref[...] = s_ref[0:BLK, a : a + BLK]

    def keep(rows, at, value):
        u_ref[rows, at] = value
        parts = split(value)
        for p in range(3):
            u3_ref[p, rows, at] = parts[p]
        return parts

    def block_copy(m):
        at = pl.ds(BLK * m, BLK)
        return pltpu.make_async_copy(u_ref.at[at, :], u_out.at[at, :], sems.at[m])

    def first_half(k):
        a, b, c = PAN * k, PAN * k + BLK, PAN * k + PAN
        inverse = split(m_ref[...])
        upper = keep(slice(a, b), slice(b, None), dot_parts(inverse, split(s_ref[0:BLK, b:]), 1))
        corner = [part[:, 0:BLK] for part in upper]
        s_ref[BLK:, b:] = s_ref[BLK:, b:] - dot_parts(corner, upper, 0)
        d_ref[...] = s_ref[BLK:, b:c]
        block_copy(2 * k).start()
        solved = dot_parts(split(own_ref[:, 0:BLK]), inverse, 1, 1)
        y_ref[:, a:b] = solved
        own_ref[:, BLK:] = own_ref[:, BLK:] - dot_parts(split(solved), corner, 1)

    def second_half(k):
        b, c = PAN * k + BLK, PAN * k + PAN
        inverse = split(m_ref[...])
        if c < width:
            keep(slice(b, c), slice(c, None), dot_parts(inverse, split(s_ref[BLK:, c:]), 1))
        block_copy(2 * k + 1).start()
        y_ref[:, b:c] = dot_parts(split(own_ref[:, BLK:]), inverse, 1, 1)
        if c < width:
            start_panel(k + 1)

    start_panel(0)

    def block(m, carry):
        at = pl.ds(pl.multiple_of(m * BLK, BLK), BLK)
        factor_block(d_ref, u_ref.at[at, at], m_ref)
        for i in range(width // BLK):

            @pl.when(m == i)
            def _():
                (second_half if i % 2 else first_half)(i // 2)

        return carry

    lax.fori_loop(0, width // BLK, block, 0)
    squares = y_ref[...] * y_ref[...]
    quad = sum(squares[:, c : c + BLK] for c in range(0, width, BLK))
    quad_ref[...] = jnp.sum(quad.T, axis=0, keepdims=True) * (1.0 / width)
    for m in range(width // BLK):
        block_copy(m).wait()


def factor_and_solve(pieces, replica):
    n_rep = len(pieces)
    height, tokens = pieces[0].shape
    width = ((height - 16) // 2) ** 2
    docs = n_rep * BAL
    return pl.pallas_call(
        functools.partial(factor_kernel, width),
        out_shape=[
            jax.ShapeDtypeStruct((width, width), jnp.float32),
            jax.ShapeDtypeStruct((BAL, width), jnp.bfloat16),
            jax.ShapeDtypeStruct((1, BAL), jnp.float32),
        ],
        in_specs=[pl.BlockSpec(memory_space=pltpu.SMEM)] + [VMEM] * n_rep,
        out_specs=[pl.BlockSpec(memory_space=pl.ANY), VMEM, VMEM],
        scratch_shapes=[
            pltpu.VMEM((n_rep, height, tokens), jnp.bfloat16),
            pltpu.VMEM((width, docs), jnp.float32),
            pltpu.VMEM((16, docs), jnp.float32),
            pltpu.VMEM((docs, 4 * tokens), jnp.bfloat16),
            pltpu.VMEM((width, docs), jnp.bfloat16),
            pltpu.VMEM((width, width), jnp.float32),
            pltpu.VMEM((3, width, width), jnp.bfloat16),
            pltpu.VMEM((PAN, width), jnp.float32),
            pltpu.VMEM((BAL, width), jnp.float32),
            pltpu.VMEM((BAL, PAN), jnp.float32),
            pltpu.VMEM((BLK, BLK), jnp.float32),
            pltpu.VMEM((BLK, BLK), jnp.float32),
            pltpu.SemaphoreType.DMA((width // BLK,)),
        ],
        compiler_params=pltpu.CompilerParams(vmem_limit_bytes=48 * 1024 * 1024),
        name="factor",
    )(jnp.reshape(replica, (1,)).astype(jnp.int32), *pieces)


def on_device(activations, output_grads, in_projection, out_projection, segment_ids, move_list):
    tokens = project(
        activations[0], output_grads[0], in_projection[0], out_projection[0], segment_ids, move_list
    )
    upper, mine, quad = factor_and_solve(gathered(tokens, "rep"), lax.axis_index("rep"))
    layers = [quad] + [swapped(quad, "layer", d) for d in range(1, lax.axis_size("layer"))]
    while len(layers) > 1:
        layers = [layers[i] + layers[i + 1] for i in range(0, len(layers), 2)]
    return (upper[None], mine[None], layers[0][0])


def solution(mesh):
    placed = (
        P("layer", "rep", None),
        P("layer", "rep", None),
        P("layer", None, None),
        P("layer", None, None),
        P("rep"),
        P("rep"),
    )
    return jax.shard_map(
        on_device,
        mesh=mesh,
        in_specs=placed,
        out_specs=(P("layer", None, None), P("layer", "rep", None), P("rep")),
        check_vma=False,
    )
```

```python
import functools

import jax
import jax.numpy as jnp
from jax import lax
from jax.experimental import pallas as pl
from jax.experimental.pallas import tpu as pltpu
from jax.sharding import PartitionSpec as P

BAL = 32
DAMPING = 0.05
BLK = 128
PAN = 256
SUP = 64
EXACT = lax.Precision.HIGHEST
VMEM = pl.BlockSpec(memory_space=pltpu.VMEM)
FAR = pl.BlockSpec(memory_space=pltpu.HBM)


def swapped(block, axis, distance):
    devices = range(lax.axis_size(axis))
    return lax.ppermute(block, axis, [(i, i ^ distance) for i in devices])


def gathered(block, axis):
    even = [swapped(block, axis, d) for d in range(2, lax.axis_size(axis), 2)]
    pieces = [block, swapped(block, axis, 1)]
    for piece in even:
        pieces += [piece, swapped(piece, axis, 1)]
    return pieces


def lane_of(v, j):
    return jnp.take_along_axis(v, jnp.full(v.shape, j, jnp.int32), axis=1)


def row_of(v, s):
    return jnp.broadcast_to(v[s : s + 1, :], v.shape)


def dot_t(a, b):
    return lax.dot_general(
        a, b, (((0,), (0,)), ((), ())), precision=EXACT, preferred_element_type=jnp.float32
    )


def split(x):
    high = x.astype(jnp.bfloat16)
    rest = x - high.astype(jnp.float32)
    middle = rest.astype(jnp.bfloat16)
    return high, middle, (rest - middle.astype(jnp.float32)).astype(jnp.bfloat16)


def dot_parts(a, b, dim_a, dim_b=0):
    left = jnp.concatenate([a[2], a[1], a[0], a[1], a[0], a[0]], dim_a)
    right = jnp.concatenate([b[0], b[1], b[2], b[0], b[1], b[0]], dim_b)
    dims = (((dim_a,), (dim_b,)), ((), ()))
    return lax.dot_general(left, right, dims, preferred_element_type=jnp.float32)


def dot_n(a, b):
    return lax.dot_general(a, b, (((1,), (1,)), ((), ())), preferred_element_type=jnp.float32)


def project_kernel(acts, grads, w_in, w_out, segments, moves, out, a_ref, g_ref, wi_ref, wo_ref, seg_ref, move_ref, sems):
    tokens, depth = a_ref.shape
    parts = sems.shape[0] // 2 - 2
    deep = depth // parts
    width = w_in.shape[0]
    small = [
        pltpu.make_async_copy(segments, seg_ref, sems.at[2 * parts]),
        pltpu.make_async_copy(moves, move_ref, sems.at[2 * parts + 1]),
    ]
    weights = [
        pltpu.make_async_copy(w_in, wi_ref, sems.at[2 * parts + 2]),
        pltpu.make_async_copy(w_out, wo_ref, sems.at[2 * parts + 3]),
    ]
    copies = []
    for c in range(parts):
        at = pl.ds(c * deep, deep)
        copies += [
            pltpu.make_async_copy(acts.at[:, at], a_ref.at[:, at], sems.at[2 * c]),
            pltpu.make_async_copy(grads.at[:, at], g_ref.at[:, at], sems.at[2 * c + 1]),
        ]
    for copy in [*small, *weights, *copies]:
        copy.start()
    for copy in small:
        copy.wait()
    slots = moves.shape[1]
    slot = lax.broadcasted_iota(jnp.int32, (slots, slots), 0)
    other = lax.broadcasted_iota(jnp.int32, (slots, slots), 1)
    column = jnp.sum(jnp.where(slot == other, move_ref[...], 0), axis=1, keepdims=True)
    segment = seg_ref[...]
    slot = lax.broadcasted_iota(jnp.int32, (slots, tokens), 0)
    target = jnp.sum(jnp.where(slot == segment, column, 0), axis=0, keepdims=True)
    target = jnp.where(segment < 0, -1, target)
    line = lax.broadcasted_iota(jnp.int32, (16, tokens), 0)
    coded = jnp.where(line == 0, target >> 5, jnp.where(line == 1, target & 31, 0))
    out[2 * width :, :] = coded.astype(jnp.float32).astype(jnp.bfloat16)
    for copy in weights:
        copy.wait()
    left = right = jnp.zeros((tokens, width), jnp.float32)
    for c in range(parts):
        at = slice(c * deep, c * deep + deep)
        copies[2 * c].wait()
        copies[2 * c + 1].wait()
        left = left + dot_n(a_ref[:, at], wi_ref[:, at])
        right = right + dot_n(g_ref[:, at], wo_ref[:, at])
    out[0:width, :] = left.T.astype(jnp.bfloat16)
    out[width : 2 * width, :] = right.T.astype(jnp.bfloat16)


def project(activations, output_grads, in_projection, out_projection, segment_ids, move_list):
    tokens, depth = activations.shape
    width = in_projection.shape[0]
    slots = move_list.shape[0]
    parts = depth // 512
    return pl.pallas_call(
        project_kernel,
        out_shape=jax.ShapeDtypeStruct((2 * width + 16, tokens), jnp.bfloat16),
        in_specs=[FAR] * 6,
        out_specs=VMEM,
        scratch_shapes=[
            pltpu.VMEM((tokens, depth), jnp.bfloat16),
            pltpu.VMEM((tokens, depth), jnp.bfloat16),
            pltpu.VMEM((width, depth), jnp.bfloat16),
            pltpu.VMEM((width, depth), jnp.bfloat16),
            pltpu.VMEM((1, tokens), jnp.int32),
            pltpu.VMEM((1, slots), jnp.int32),
            pltpu.SemaphoreType.DMA((2 * parts + 4,)),
        ],
        compiler_params=pltpu.CompilerParams(vmem_limit_bytes=58 * 1024 * 1024),
        name="project",
    )(
        activations,
        output_grads,
        in_projection,
        out_projection,
        segment_ids.reshape(1, tokens),
        move_list.reshape(1, slots),
    )


def eliminate(x, first):
    lane = lax.broadcasted_iota(jnp.int32, (8, BLK), 1)
    sub = lax.broadcasted_iota(jnp.int32, (8, BLK), 0)
    x, count = list(x), len(x)
    scales = [None] * count
    spread = lambda group, lo: [lane_of(group, lo + c) for c in range(8)]
    cols = spread(x[0], first)
    pivot = row_of(cols[0], 0)
    for t in range(count):
        lo = first + 8 * t
        work = x[t]
        more = t + 1 < count
        if more:
            below = [spread(x[i], lo) for i in range(t + 1, count)]
            ahead = spread(x[t + 1], lo + 8)
            factor = list(below[0])
        kept, pivots = work, jnp.ones((8, BLK), jnp.float32)
        for c in range(8):
            hit, at = sub == c, lane == lo + c
            inv = 1.0 / pivot
            kept = jnp.where(hit, work, kept)
            pivots = jnp.where(hit, pivot, pivots)
            other = jnp.where(hit, 0.0, cols[c])
            scaled = other * inv
            raws = {k: row_of(cols[c], k) for k in range(c + 1, 8)}
            if c < 7:
                pivot = row_of(cols[c + 1], c + 1) - (raws[c + 1] * raws[c + 1]) * inv
            elif more:
                edge = row_of(factor[7], 0)
                pivot = row_of(ahead[0], 0) - (edge * edge) * inv
            row = jnp.where(at, 1.0, row_of(work, c))
            work = jnp.where(at, jnp.where(hit, 1.0, 0.0), work) - scaled * row
            for k in range(c + 1, 8):
                cols[k] = cols[k] - scaled * raws[k]
            if more:
                part = factor[c] * inv
                for k in range(c + 1, 8):
                    factor[k] = factor[k] - part * raws[k]
                for k in range(8):
                    ahead[k] = ahead[k] - part * row_of(factor[c], k)
        work = work * (1.0 / pivots)
        if more:
            inside = (lane >= lo) & (lane < lo + 8)
            rows = [row_of(work, c) for c in range(8)]
            for i in range(t + 1, count):
                terms = [below[i - t - 1][c] * rows[c] for c in range(8)]
                while len(terms) > 1:
                    terms = [terms[m] + terms[m + 1] for m in range(0, len(terms), 2)]
                x[i] = jnp.where(inside, 0.0, x[i]) - terms[0]
            cols = ahead
        scales[t] = lax.rsqrt(pivots)
        x[t] = kept * scales[t]
    return x, scales


def factor_block(d_ref, u_ref, m_ref):
    lane = lax.broadcasted_iota(jnp.int32, (8, BLK), 1)
    sub = lax.broadcasted_iota(jnp.int32, (8, BLK), 0)
    tall_row = lax.broadcasted_iota(jnp.int32, (SUP, BLK), 0)
    tall_lane = lax.broadcasted_iota(jnp.int32, (SUP, BLK), 1)
    groups, n = BLK // 8, SUP // 8
    x = [d_ref[8 * i : 8 * i + 8, :] for i in range(groups)]
    for h in range(0, groups, n):
        a, b = 8 * h, 8 * (h + n)
        rows, scales = eliminate(x[h : h + n], a)
        if b < BLK:
            block, scale = jnp.concatenate(rows, 0), jnp.concatenate(scales, 0)
            row = tall_row + a
            right = jnp.where(
                (tall_lane > row) & (tall_lane < b), 0.0, jnp.where(tall_lane == row, scale, block)
            )
            update = dot_t(block, right)
            for i in range(h + n, groups):
                x[i] = jnp.where((lane >= a) & (lane < b), 0.0, x[i]) - update[8 * i : 8 * i + 8, :]
        for q in range(n):
            row = a + 8 * q + sub
            at = slice(a + 8 * q, a + 8 * q + 8)
            u_ref[at, :] = jnp.where(lane >= row, rows[q], 0.0)
            m_ref[at, :] = jnp.where(lane < row, rows[q], jnp.where(lane == row, scales[q], 0.0))


def factor_kernel(width, me_ref, *refs):
    *pieces, u_out, mine_out, quad_ref, tok_ref, sum_ref, len_ref, p_ref, f_ref, u_ref, u3_ref, s_ref, y_ref, own_ref, d_ref, m_ref, sems = refs
    n_rep = len(pieces)
    docs = p_ref.shape[0]
    rows = docs // n_rep
    tokens = p_ref.shape[1] // 2
    me = me_ref[0]
    for d in range(n_rep):
        tok_ref[me ^ d] = pieces[d][...]
    sum_ref[...] = jnp.zeros_like(sum_ref)
    len_ref[...] = jnp.zeros_like(len_ref)
    side = (tok_ref.shape[1] - 16) // 2
    doc = lax.broadcasted_iota(jnp.int32, (docs, tokens), 0).astype(jnp.float32)
    ones = jnp.ones((16, 2 * tokens), jnp.bfloat16)
    tall = 8 * side

    def add_tokens(pair, last):
        for h in range(2):
            coded = tok_ref[2 * pair + h, 2 * side :, :].astype(jnp.float32)
            target = coded[0:1, :] * 32.0 + coded[1:2, :]
            target = jnp.where(target < 0.0, last, target)
            last = target[:, tokens - 1 : tokens]
            member = jnp.where(doc == target, 1.0, 0.0).astype(jnp.bfloat16)
            p_ref[:, h * tokens : (h + 1) * tokens] = member
        lefts = [tok_ref[2 * pair + h, 0:side, :].astype(jnp.float32) for h in range(2)]
        rights = [tok_ref[2 * pair + h, side : 2 * side, :].astype(jnp.float32) for h in range(2)]
        for q in range(0, side, 8):
            highs, lows = [], []
            for h in range(2):
                left, right = lefts[h], rights[h]
                outer = jnp.concatenate(
                    [jnp.broadcast_to(left[i : i + 1, :], right.shape) * right for i in range(q, q + 8)], 0
                )
                highs.append(outer.astype(jnp.bfloat16))
                lows.append((outer - highs[h].astype(jnp.float32)).astype(jnp.bfloat16))
            parts = [jnp.concatenate(highs, 1), jnp.concatenate(lows, 1)]
            if q == 0:
                parts.append(ones)
            both = dot_n(jnp.concatenate(parts, 0), p_ref[...])
            if q == 0:
                len_ref[...] += both[2 * tall :]
            sum_ref[q * side : q * side + tall, :] += both[0:tall] + both[tall : 2 * tall]
        return last

    lax.fori_loop(0, n_rep // 2, add_tokens, jnp.zeros((1, 1), jnp.float32))
    scale = lax.rsqrt(jnp.maximum(len_ref[0:1, :], 1.0))
    f_ref[...] = (sum_ref[...] * scale).astype(jnp.bfloat16)
    row = lax.broadcasted_iota(jnp.int32, (rows, docs), 0)
    slot = lax.broadcasted_iota(jnp.int32, (rows, docs), 1)
    pick_t = jnp.where(slot == me * rows + row, 1.0, 0.0).astype(jnp.bfloat16)
    mine_out[...] = dot_n(pick_t, f_ref[...]).astype(jnp.bfloat16)
    eye = jnp.where(
        lax.broadcasted_iota(jnp.int32, (PAN, PAN), 0) == lax.broadcasted_iota(jnp.int32, (PAN, PAN), 1),
        DAMPING,
        0.0,
    )

    def start_panel(k):
        a, c = PAN * k, PAN * k + PAN
        s_ref[:, a:] = dot_n(f_ref[a:c, :], f_ref[a:, :]) * (1.0 / docs)
        s_ref[:, a:c] = s_ref[:, a:c] + eye
        own = mine_out[:, a:c].astype(jnp.float32)
        if k:
            done = [u3_ref[p, 0:a, a:c] for p in range(3)]
            s_ref[:, a:] = s_ref[:, a:] - dot_parts(done, [u3_ref[p, 0:a, a:] for p in range(3)], 0)
            own = own - dot_parts(split(y_ref[:, 0:a]), done, 1)
            u_ref[a:c, 0:a] = jnp.zeros((PAN, a), jnp.float32)
        own_ref[...] = own
        u_ref[a + BLK : c, a : a + BLK] = jnp.zeros((BLK, BLK), jnp.float32)
        d_ref[...] = s_ref[0:BLK, a : a + BLK]

    def keep(rows, at, value):
        u_ref[rows, at] = value
        parts = split(value)
        for p in range(3):
            u3_ref[p, rows, at] = parts[p]
        return parts

    def block_copy(m):
        at = pl.ds(BLK * m, BLK)
        return pltpu.make_async_copy(u_ref.at[at, :], u_out.at[at, :], sems.at[m])

    def first_half(k):
        a, b, c = PAN * k, PAN * k + BLK, PAN * k + PAN
        inverse = split(m_ref[...])
        upper = keep(slice(a, b), slice(b, None), dot_parts(inverse, split(s_ref[0:BLK, b:]), 1))
        corner = [part[:, 0:BLK] for part in upper]
        s_ref[BLK:, b:] = s_ref[BLK:, b:] - dot_parts(corner, upper, 0)
        d_ref[...] = s_ref[BLK:, b:c]
        block_copy(2 * k).start()
        solved = dot_parts(split(own_ref[:, 0:BLK]), inverse, 1, 1)
        y_ref[:, a:b] = solved
        own_ref[:, BLK:] = own_ref[:, BLK:] - dot_parts(split(solved), corner, 1)

    def second_half(k):
        b, c = PAN * k + BLK, PAN * k + PAN
        inverse = split(m_ref[...])
        if c < width:
            keep(slice(b, c), slice(c, None), dot_parts(inverse, split(s_ref[BLK:, c:]), 1))
        block_copy(2 * k + 1).start()
        y_ref[:, b:c] = dot_parts(split(own_ref[:, BLK:]), inverse, 1, 1)
        if c < width:
            start_panel(k + 1)

    start_panel(0)

    def block(m, carry):
        at = pl.ds(pl.multiple_of(m * BLK, BLK), BLK)
        factor_block(d_ref, u_ref.at[at, at], m_ref)
        for i in range(width // BLK):

            @pl.when(m == i)
            def _():
                (second_half if i % 2 else first_half)(i // 2)

        return carry

    lax.fori_loop(0, width // BLK, block, 0)
    squares = y_ref[...] * y_ref[...]
    quad = sum(squares[:, c : c + BLK] for c in range(0, width, BLK))
    quad_ref[...] = jnp.sum(quad.T, axis=0, keepdims=True) * (1.0 / width)
    for m in range(width // BLK):
        block_copy(m).wait()


def factor_and_solve(pieces, replica):
    n_rep = len(pieces)
    height, tokens = pieces[0].shape
    width = ((height - 16) // 2) ** 2
    docs = n_rep * BAL
    return pl.pallas_call(
        functools.partial(factor_kernel, width),
        out_shape=[
            jax.ShapeDtypeStruct((width, width), jnp.float32),
            jax.ShapeDtypeStruct((BAL, width), jnp.bfloat16),
            jax.ShapeDtypeStruct((1, BAL), jnp.float32),
        ],
        in_specs=[pl.BlockSpec(memory_space=pltpu.SMEM)] + [VMEM] * n_rep,
        out_specs=[pl.BlockSpec(memory_space=pl.ANY), VMEM, VMEM],
        scratch_shapes=[
            pltpu.VMEM((n_rep, height, tokens), jnp.bfloat16),
            pltpu.VMEM((width, docs), jnp.float32),
            pltpu.VMEM((16, docs), jnp.float32),
            pltpu.VMEM((docs, 2 * tokens), jnp.bfloat16),
            pltpu.VMEM((width, docs), jnp.bfloat16),
            pltpu.VMEM((width, width), jnp.float32),
            pltpu.VMEM((3, width, width), jnp.bfloat16),
            pltpu.VMEM((PAN, width), jnp.float32),
            pltpu.VMEM((BAL, width), jnp.float32),
            pltpu.VMEM((BAL, PAN), jnp.float32),
            pltpu.VMEM((BLK, BLK), jnp.float32),
            pltpu.VMEM((BLK, BLK), jnp.float32),
            pltpu.SemaphoreType.DMA((width // BLK,)),
        ],
        compiler_params=pltpu.CompilerParams(vmem_limit_bytes=48 * 1024 * 1024),
        name="factor",
    )(jnp.reshape(replica, (1,)).astype(jnp.int32), *pieces)


def on_device(activations, output_grads, in_projection, out_projection, segment_ids, move_list):
    tokens = project(
        activations[0], output_grads[0], in_projection[0], out_projection[0], segment_ids, move_list
    )
    upper, mine, quad = factor_and_solve(gathered(tokens, "rep"), lax.axis_index("rep"))
    layers = [quad] + [swapped(quad, "layer", d) for d in range(1, lax.axis_size("layer"))]
    while len(layers) > 1:
        layers = [layers[i] + layers[i + 1] for i in range(0, len(layers), 2)]
    return (upper[None], mine[None], layers[0][0])


def solution(mesh):
    placed = (
        P("layer", "rep", None),
        P("layer", "rep", None),
        P("layer", None, None),
        P("layer", None, None),
        P("rep"),
        P("rep"),
    )
    return jax.shard_map(
        on_device,
        mesh=mesh,
        in_specs=placed,
        out_specs=(P("layer", None, None), P("layer", "rep", None), P("rep")),
        check_vma=False,
    )
```

```python
import functools

import jax
import jax.numpy as jnp
from jax import lax
from jax.experimental import pallas as pl
from jax.experimental.pallas import tpu as pltpu
from jax.sharding import PartitionSpec as P

BAL = 32
DAMPING = 0.05
BLK = 128
PAN = 256
SUP = 64
EXACT = lax.Precision.HIGHEST
VMEM = pl.BlockSpec(memory_space=pltpu.VMEM)
FAR = pl.BlockSpec(memory_space=pltpu.HBM)


def swapped(block, axis, distance):
    devices = range(lax.axis_size(axis))
    return lax.ppermute(block, axis, [(i, i ^ distance) for i in devices])


def gathered(block, axis):
    even = [swapped(block, axis, d) for d in range(2, lax.axis_size(axis), 2)]
    pieces = [block, swapped(block, axis, 1)]
    for piece in even:
        pieces += [piece, swapped(piece, axis, 1)]
    return pieces


def lane_of(v, j):
    return jnp.take_along_axis(v, jnp.full(v.shape, j, jnp.int32), axis=1)


def row_of(v, s):
    return jnp.broadcast_to(v[s : s + 1, :], v.shape)


def dot_t(a, b):
    return lax.dot_general(
        a, b, (((0,), (0,)), ((), ())), precision=EXACT, preferred_element_type=jnp.float32
    )


def split(x):
    high = x.astype(jnp.bfloat16)
    rest = x - high.astype(jnp.float32)
    middle = rest.astype(jnp.bfloat16)
    return high, middle, (rest - middle.astype(jnp.float32)).astype(jnp.bfloat16)


def dot_parts(a, b, dim_a, dim_b=0):
    left = jnp.concatenate([a[2], a[1], a[0], a[1], a[0], a[0]], dim_a)
    right = jnp.concatenate([b[0], b[1], b[2], b[0], b[1], b[0]], dim_b)
    dims = (((dim_a,), (dim_b,)), ((), ()))
    return lax.dot_general(left, right, dims, preferred_element_type=jnp.float32)


def dot_n(a, b):
    return lax.dot_general(a, b, (((1,), (1,)), ((), ())), preferred_element_type=jnp.float32)


def project_kernel(acts, grads, w_in, w_out, segments, moves, out, a_ref, g_ref, wi_ref, wo_ref, seg_ref, move_ref, sems):
    tokens, depth = a_ref.shape
    parts = sems.shape[0] // 2 - 2
    deep = depth // parts
    width = w_in.shape[0]
    small = [
        pltpu.make_async_copy(segments, seg_ref, sems.at[2 * parts]),
        pltpu.make_async_copy(moves, move_ref, sems.at[2 * parts + 1]),
    ]
    weights = [
        pltpu.make_async_copy(w_in, wi_ref, sems.at[2 * parts + 2]),
        pltpu.make_async_copy(w_out, wo_ref, sems.at[2 * parts + 3]),
    ]
    copies = []
    for c in range(parts):
        at = pl.ds(c * deep, deep)
        copies += [
            pltpu.make_async_copy(acts.at[:, at], a_ref.at[:, at], sems.at[2 * c]),
            pltpu.make_async_copy(grads.at[:, at], g_ref.at[:, at], sems.at[2 * c + 1]),
        ]
    for copy in [*small, *weights, *copies]:
        copy.start()
    for copy in small:
        copy.wait()
    slots = moves.shape[1]
    slot = lax.broadcasted_iota(jnp.int32, (slots, slots), 0)
    other = lax.broadcasted_iota(jnp.int32, (slots, slots), 1)
    column = jnp.sum(jnp.where(slot == other, move_ref[...], 0), axis=1, keepdims=True)
    segment = seg_ref[...]
    slot = lax.broadcasted_iota(jnp.int32, (slots, tokens), 0)
    target = jnp.sum(jnp.where(slot == segment, column, 0), axis=0, keepdims=True)
    target = jnp.where(segment < 0, -1, target)
    line = lax.broadcasted_iota(jnp.int32, (16, tokens), 0)
    coded = jnp.where(line == 0, target >> 5, jnp.where(line == 1, target & 31, 0))
    out[2 * width :, :] = coded.astype(jnp.float32).astype(jnp.bfloat16)
    for copy in weights:
        copy.wait()
    left = right = jnp.zeros((tokens, width), jnp.float32)
    for c in range(parts):
        at = slice(c * deep, c * deep + deep)
        copies[2 * c].wait()
        copies[2 * c + 1].wait()
        left = left + dot_n(a_ref[:, at], wi_ref[:, at])
        right = right + dot_n(g_ref[:, at], wo_ref[:, at])
    out[0:width, :] = left.T.astype(jnp.bfloat16)
    out[width : 2 * width, :] = right.T.astype(jnp.bfloat16)


def project(activations, output_grads, in_projection, out_projection, segment_ids, move_list):
    tokens, depth = activations.shape
    width = in_projection.shape[0]
    slots = move_list.shape[0]
    parts = depth // 512
    return pl.pallas_call(
        project_kernel,
        out_shape=jax.ShapeDtypeStruct((2 * width + 16, tokens), jnp.bfloat16),
        in_specs=[FAR] * 6,
        out_specs=VMEM,
        scratch_shapes=[
            pltpu.VMEM((tokens, depth), jnp.bfloat16),
            pltpu.VMEM((tokens, depth), jnp.bfloat16),
            pltpu.VMEM((width, depth), jnp.bfloat16),
            pltpu.VMEM((width, depth), jnp.bfloat16),
            pltpu.VMEM((1, tokens), jnp.int32),
            pltpu.VMEM((1, slots), jnp.int32),
            pltpu.SemaphoreType.DMA((2 * parts + 4,)),
        ],
        compiler_params=pltpu.CompilerParams(vmem_limit_bytes=58 * 1024 * 1024),
        name="project",
    )(
        activations,
        output_grads,
        in_projection,
        out_projection,
        segment_ids.reshape(1, tokens),
        move_list.reshape(1, slots),
    )


def eliminate(x, first):
    lane = lax.broadcasted_iota(jnp.int32, (8, BLK), 1)
    sub = lax.broadcasted_iota(jnp.int32, (8, BLK), 0)
    x, count = list(x), len(x)
    scales = [None] * count
    spread = lambda group, lo: [lane_of(group, lo + c) for c in range(8)]
    cols = spread(x[0], first)
    pivot = row_of(cols[0], 0)
    for t in range(count):
        lo = first + 8 * t
        work = x[t]
        more = t + 1 < count
        if more:
            below = [spread(x[i], lo) for i in range(t + 1, count)]
            ahead = spread(x[t + 1], lo + 8)
            factor = list(below[0])
        kept, pivots = work, jnp.ones((8, BLK), jnp.float32)
        for c in range(8):
            hit, at = sub == c, lane == lo + c
            inv = 1.0 / pivot
            kept = jnp.where(hit, work, kept)
            pivots = jnp.where(hit, pivot, pivots)
            other = jnp.where(hit, 0.0, cols[c])
            scaled = other * inv
            raws = {k: row_of(cols[c], k) for k in range(c + 1, 8)}
            if c < 7:
                pivot = row_of(cols[c + 1], c + 1) - (raws[c + 1] * raws[c + 1]) * inv
            elif more:
                edge = row_of(factor[7], 0)
                pivot = row_of(ahead[0], 0) - (edge * edge) * inv
            row = jnp.where(at, 1.0, row_of(work, c))
            work = jnp.where(at, jnp.where(hit, 1.0, 0.0), work) - scaled * row
            for k in range(c + 1, 8):
                cols[k] = cols[k] - scaled * raws[k]
            if more:
                part = factor[c] * inv
                for k in range(c + 1, 8):
                    factor[k] = factor[k] - part * raws[k]
                for k in range(8):
                    ahead[k] = ahead[k] - part * row_of(factor[c], k)
        work = work * (1.0 / pivots)
        if more:
            inside = (lane >= lo) & (lane < lo + 8)
            rows = [row_of(work, c) for c in range(8)]
            for i in range(t + 1, count):
                terms = [below[i - t - 1][c] * rows[c] for c in range(8)]
                while len(terms) > 1:
                    terms = [terms[m] + terms[m + 1] for m in range(0, len(terms), 2)]
                x[i] = jnp.where(inside, 0.0, x[i]) - terms[0]
            cols = ahead
        scales[t] = lax.rsqrt(pivots)
        x[t] = kept * scales[t]
    return x, scales


def factor_block(d_ref, u_ref, m_ref):
    lane = lax.broadcasted_iota(jnp.int32, (8, BLK), 1)
    sub = lax.broadcasted_iota(jnp.int32, (8, BLK), 0)
    tall_row = lax.broadcasted_iota(jnp.int32, (SUP, BLK), 0)
    tall_lane = lax.broadcasted_iota(jnp.int32, (SUP, BLK), 1)
    groups, n = BLK // 8, SUP // 8
    x = [d_ref[8 * i : 8 * i + 8, :] for i in range(groups)]
    for h in range(0, groups, n):
        a, b = 8 * h, 8 * (h + n)
        rows, scales = eliminate(x[h : h + n], a)
        if b < BLK:
            block, scale = jnp.concatenate(rows, 0), jnp.concatenate(scales, 0)
            row = tall_row + a
            right = jnp.where(
                (tall_lane > row) & (tall_lane < b), 0.0, jnp.where(tall_lane == row, scale, block)
            )
            update = dot_parts(split(block), split(right), 0)
            for i in range(h + n, groups):
                x[i] = jnp.where((lane >= a) & (lane < b), 0.0, x[i]) - update[8 * i : 8 * i + 8, :]
        for q in range(n):
            row = a + 8 * q + sub
            at = slice(a + 8 * q, a + 8 * q + 8)
            u_ref[at, :] = jnp.where(lane >= row, rows[q], 0.0)
            m_ref[at, :] = jnp.where(lane < row, rows[q], jnp.where(lane == row, scales[q], 0.0))


def factor_kernel(width, me_ref, *refs):
    *pieces, u_out, mine_out, quad_ref, tok_ref, sum_ref, len_ref, p_ref, f_ref, u_ref, u3_ref, s_ref, y_ref, own_ref, d_ref, m_ref, sems = refs
    n_rep = len(pieces)
    docs = p_ref.shape[0]
    rows = docs // n_rep
    tokens = p_ref.shape[1] // 2
    me = me_ref[0]
    for d in range(n_rep):
        tok_ref[me ^ d] = pieces[d][...]
    sum_ref[...] = jnp.zeros_like(sum_ref)
    len_ref[...] = jnp.zeros_like(len_ref)
    side = (tok_ref.shape[1] - 16) // 2
    doc = lax.broadcasted_iota(jnp.int32, (docs, tokens), 0).astype(jnp.float32)
    ones = jnp.ones((16, 2 * tokens), jnp.bfloat16)
    tall = 8 * side

    def add_tokens(pair, last):
        for h in range(2):
            coded = tok_ref[2 * pair + h, 2 * side :, :].astype(jnp.float32)
            target = coded[0:1, :] * 32.0 + coded[1:2, :]
            target = jnp.where(target < 0.0, last, target)
            last = target[:, tokens - 1 : tokens]
            member = jnp.where(doc == target, 1.0, 0.0).astype(jnp.bfloat16)
            p_ref[:, h * tokens : (h + 1) * tokens] = member
        lefts = [tok_ref[2 * pair + h, 0:side, :].astype(jnp.float32) for h in range(2)]
        rights = [tok_ref[2 * pair + h, side : 2 * side, :].astype(jnp.float32) for h in range(2)]
        for q in range(0, side, 8):
            highs, lows = [], []
            for h in range(2):
                left, right = lefts[h], rights[h]
                outer = jnp.concatenate(
                    [jnp.broadcast_to(left[i : i + 1, :], right.shape) * right for i in range(q, q + 8)], 0
                )
                highs.append(outer.astype(jnp.bfloat16))
                lows.append((outer - highs[h].astype(jnp.float32)).astype(jnp.bfloat16))
            parts = [jnp.concatenate(highs, 1), jnp.concatenate(lows, 1)]
            if q == 0:
                parts.append(ones)
            both = dot_n(jnp.concatenate(parts, 0), p_ref[...])
            if q == 0:
                len_ref[...] += both[2 * tall :]
            sum_ref[q * side : q * side + tall, :] += both[0:tall] + both[tall : 2 * tall]
        return last

    lax.fori_loop(0, n_rep // 2, add_tokens, jnp.zeros((1, 1), jnp.float32))
    scale = lax.rsqrt(jnp.maximum(len_ref[0:1, :], 1.0))
    f_ref[...] = (sum_ref[...] * scale).astype(jnp.bfloat16)
    row = lax.broadcasted_iota(jnp.int32, (rows, docs), 0)
    slot = lax.broadcasted_iota(jnp.int32, (rows, docs), 1)
    pick_t = jnp.where(slot == me * rows + row, 1.0, 0.0).astype(jnp.bfloat16)
    mine_out[...] = dot_n(pick_t, f_ref[...]).astype(jnp.bfloat16)
    eye = jnp.where(
        lax.broadcasted_iota(jnp.int32, (PAN, PAN), 0) == lax.broadcasted_iota(jnp.int32, (PAN, PAN), 1),
        DAMPING,
        0.0,
    )

    def start_panel(k):
        a, c = PAN * k, PAN * k + PAN
        s_ref[:, a:] = dot_n(f_ref[a:c, :], f_ref[a:, :]) * (1.0 / docs)
        s_ref[:, a:c] = s_ref[:, a:c] + eye
        own = mine_out[:, a:c].astype(jnp.float32)
        if k:
            done = [u3_ref[p, 0:a, a:c] for p in range(3)]
            s_ref[:, a:] = s_ref[:, a:] - dot_parts(done, [u3_ref[p, 0:a, a:] for p in range(3)], 0)
            own = own - dot_parts(split(y_ref[:, 0:a]), done, 1)
            u_ref[a:c, 0:a] = jnp.zeros((PAN, a), jnp.float32)
        own_ref[...] = own
        u_ref[a + BLK : c, a : a + BLK] = jnp.zeros((BLK, BLK), jnp.float32)
        d_ref[...] = s_ref[0:BLK, a : a + BLK]

    def keep(rows, at, value):
        u_ref[rows, at] = value
        parts = split(value)
        for p in range(3):
            u3_ref[p, rows, at] = parts[p]
        return parts

    def block_copy(m):
        at = pl.ds(BLK * m, BLK)
        return pltpu.make_async_copy(u_ref.at[at, :], u_out.at[at, :], sems.at[m])

    def first_half(k):
        a, b, c = PAN * k, PAN * k + BLK, PAN * k + PAN
        inverse = split(m_ref[...])
        upper = keep(slice(a, b), slice(b, None), dot_parts(inverse, split(s_ref[0:BLK, b:]), 1))
        corner = [part[:, 0:BLK] for part in upper]
        s_ref[BLK:, b:] = s_ref[BLK:, b:] - dot_parts(corner, upper, 0)
        d_ref[...] = s_ref[BLK:, b:c]
        block_copy(2 * k).start()
        solved = dot_parts(split(own_ref[:, 0:BLK]), inverse, 1, 1)
        y_ref[:, a:b] = solved
        own_ref[:, BLK:] = own_ref[:, BLK:] - dot_parts(split(solved), corner, 1)

    def second_half(k):
        b, c = PAN * k + BLK, PAN * k + PAN
        inverse = split(m_ref[...])
        if c < width:
            keep(slice(b, c), slice(c, None), dot_parts(inverse, split(s_ref[BLK:, c:]), 1))
        block_copy(2 * k + 1).start()
        y_ref[:, b:c] = dot_parts(split(own_ref[:, BLK:]), inverse, 1, 1)
        if c < width:
            start_panel(k + 1)

    start_panel(0)

    def block(m, carry):
        at = pl.ds(pl.multiple_of(m * BLK, BLK), BLK)
        factor_block(d_ref, u_ref.at[at, at], m_ref)
        for i in range(width // BLK):

            @pl.when(m == i)
            def _():
                (second_half if i % 2 else first_half)(i // 2)

        return carry

    lax.fori_loop(0, width // BLK, block, 0)
    squares = y_ref[...] * y_ref[...]
    quad = sum(squares[:, c : c + BLK] for c in range(0, width, BLK))
    quad_ref[...] = jnp.sum(quad.T, axis=0, keepdims=True) * (1.0 / width)
    for m in range(width // BLK):
        block_copy(m).wait()


def factor_and_solve(pieces, replica):
    n_rep = len(pieces)
    height, tokens = pieces[0].shape
    width = ((height - 16) // 2) ** 2
    docs = n_rep * BAL
    return pl.pallas_call(
        functools.partial(factor_kernel, width),
        out_shape=[
            jax.ShapeDtypeStruct((width, width), jnp.float32),
            jax.ShapeDtypeStruct((BAL, width), jnp.bfloat16),
            jax.ShapeDtypeStruct((1, BAL), jnp.float32),
        ],
        in_specs=[pl.BlockSpec(memory_space=pltpu.SMEM)] + [VMEM] * n_rep,
        out_specs=[pl.BlockSpec(memory_space=pl.ANY), VMEM, VMEM],
        scratch_shapes=[
            pltpu.VMEM((n_rep, height, tokens), jnp.bfloat16),
            pltpu.VMEM((width, docs), jnp.float32),
            pltpu.VMEM((16, docs), jnp.float32),
            pltpu.VMEM((docs, 2 * tokens), jnp.bfloat16),
            pltpu.VMEM((width, docs), jnp.bfloat16),
            pltpu.VMEM((width, width), jnp.float32),
            pltpu.VMEM((3, width, width), jnp.bfloat16),
            pltpu.VMEM((PAN, width), jnp.float32),
            pltpu.VMEM((BAL, width), jnp.float32),
            pltpu.VMEM((BAL, PAN), jnp.float32),
            pltpu.VMEM((BLK, BLK), jnp.float32),
            pltpu.VMEM((BLK, BLK), jnp.float32),
            pltpu.SemaphoreType.DMA((width // BLK,)),
        ],
        compiler_params=pltpu.CompilerParams(vmem_limit_bytes=48 * 1024 * 1024),
        name="factor",
    )(jnp.reshape(replica, (1,)).astype(jnp.int32), *pieces)


def on_device(activations, output_grads, in_projection, out_projection, segment_ids, move_list):
    tokens = project(
        activations[0], output_grads[0], in_projection[0], out_projection[0], segment_ids, move_list
    )
    upper, mine, quad = factor_and_solve(gathered(tokens, "rep"), lax.axis_index("rep"))
    layers = [quad] + [swapped(quad, "layer", d) for d in range(1, lax.axis_size("layer"))]
    while len(layers) > 1:
        layers = [layers[i] + layers[i + 1] for i in range(0, len(layers), 2)]
    return (upper[None], mine[None], layers[0][0])


def solution(mesh):
    placed = (
        P("layer", "rep", None),
        P("layer", "rep", None),
        P("layer", None, None),
        P("layer", None, None),
        P("rep"),
        P("rep"),
    )
    return jax.shard_map(
        on_device,
        mesh=mesh,
        in_specs=placed,
        out_specs=(P("layer", None, None), P("layer", "rep", None), P("rep")),
        check_vma=False,
    )
```
